32 devices in a mesh: replica: 8 (over y, x, core), tensor: 4 (over z).
Axes of the slice: x: 2, y: 2, z: 4, core: 2. Of those that a mesh axis runs over, the one named last changes fastest.
Arguments:
- hidden: bfloat16 [2048, 7168], P('replica', 'tensor'), may hold values from -6 to 6
- out_grad: bfloat16 [2048, 4096], P(('replica', 'tensor')), may hold values from -6 to 6
- weights: bfloat16 [8, 56, 128, 1024], P('replica', 'tensor'), may hold values from -6 to 6
- momentum: bfloat16 [8, 56, 128, 1024], P('replica', 'tensor'), may hold values from -3 to 3
- block_cols: int32 [56, 8], P('tensor'), may hold values from 0 to 31, as said below
- step_number: int32 [1], replicated, may hold values from 0 to 999
Outputs:
- outputs: bfloat16 [2048, 4096], P(('replica', 'tensor'))
- new_weights: bfloat16 [8, 56, 128, 1024], P('replica', 'tensor')
- new_momentum: bfloat16 [8, 56, 128, 1024], P('replica', 'tensor')
The draws below stay inside these ranges and needn't reach their ends.
Inputs may be any that keep to these rules, and one draw needn't show every extreme that they name: `block_cols`: each row names 8 different column blocks; all replicas share the pattern.
All inputs are finite; a program needn't handle non-finite values.
Results may differ from the reference program's by a relative error of at most 0.013.
Values may be sent and summed in bfloat16 or wider, within the bound.
No kernel may reach another device: no remote copies, remote signals or barrier semaphores. Data moves between devices by JAX's collectives and lax.ppermute only.
A program may use at most 192 MiB of HBM per device.

```python
import jax
import jax.numpy as jnp
from jax import lax

D = 4096
BLOCK = 128
TOK = 256
KB = 8
FF = 7168
TOKENS = 2048
N_REPLICA = 8
N_TENSOR = 4


def draw_block_cols(key, part):
    row_total = FF // BLOCK
    keys = jax.random.split(jax.random.fold_in(key, 17), row_total)

    def pick_row(row_key):
        return jax.random.permutation(row_key, D // BLOCK)[:KB]
    return jax.vmap(pick_row)(keys).astype(jnp.int32)


def level_of(own_key, dims, cuts, smallest, high):
    factor_of, own = 1.0, jax.random.fold_in(own_key, 6)
    for axis_at, shards_of in cuts:
        draws = jnp.exp(jax.random.uniform(jax.random.fold_in(own, axis_at), (shards_of,), jnp.float32, smallest / len(cuts), high / len(cuts)))
        factor_of = factor_of * jnp.repeat(draws, dims[axis_at] // shards_of).reshape([-1 if axis == axis_at else 1 for axis in range(len(dims))])
    return factor_of


def scatter_about(key, shape, deviation, limit, cuts=(), held_as=jnp.bfloat16):
    drawn = deviation * jax.random.normal(key, shape, jnp.float32)
    if cuts:
        drawn = drawn * level_of(key, shape, cuts, -0.22, 0.18)
    return jnp.clip(drawn, -limit, limit).astype(held_as)


def setup_inputs(seed: int = 0) -> dict:
    key_of = jax.random.split(jax.random.key(seed), 7)
    return {
        "hidden": scatter_about(key_of[0], (TOKENS, FF), 1.0, 6.0, ((0, 8), (1, 4))),
        "out_grad": scatter_about(key_of[1], (TOKENS, D), 1.0, 6.0, ((0, 32),)),
        "weights": scatter_about(key_of[2], (N_REPLICA, FF // BLOCK, BLOCK, KB * BLOCK), 1.0, 6.0, ((0, 8), (1, 4))),
        "momentum": scatter_about(key_of[3], (N_REPLICA, FF // BLOCK, BLOCK, KB * BLOCK), 0.5, 3.0, ((0, 8), (1, 4))),
        "block_cols": draw_block_cols(jax.random.fold_in(key_of[6], 71), 0),
        "step_number": jax.random.randint(key_of[5], (1,), 0, 1000).astype(jnp.int32),
    }


LAMBDA_DC = 1.0
MOMENT_DECAY = 0.9
LEARN_RATE = 0.2


def replica_pass(hidden_rows, grad_rows, local_weights, block_cols, weight_scale):
    col_blocks = D // BLOCK
    row_total = FF // BLOCK
    hid_blocks = hidden_rows.reshape(TOK, row_total, BLOCK)
    grad_blocks = grad_rows.reshape(TOK, col_blocks, BLOCK)

    def row_block(position):
        hid_piece = lax.dynamic_index_in_dim(hid_blocks, position, 1, keepdims=False)
        weight_piece = lax.dynamic_index_in_dim(local_weights, position, 0, keepdims=False)
        columns = lax.dynamic_index_in_dim(block_cols, position, 0, keepdims=False)
        product = jnp.dot(hid_piece, weight_piece, preferred_element_type=jnp.float32) * weight_scale
        selected = jnp.take(grad_blocks, columns, axis=1).reshape(TOK, KB * BLOCK)
        gradient = jnp.dot(hid_piece.T, selected, preferred_element_type=jnp.float32)
        return product, gradient

    products, gradients = lax.map(row_block, jnp.arange(row_total, dtype=jnp.int32))
    moved = products.reshape(row_total, TOK, KB, BLOCK).transpose(0, 2, 1, 3)
    shard_of = (jnp.arange(row_total, dtype=jnp.int32) // (row_total // N_TENSOR))[:, None]
    parts = jnp.zeros((N_TENSOR, col_blocks, TOK, BLOCK), jnp.float32).at[shard_of, block_cols].add(moved)
    parts = lax.optimization_barrier(parts.astype(jnp.bfloat16)).astype(jnp.float32)
    summed = jnp.sum(parts, axis=0).transpose(1, 0, 2).reshape(TOK, D)
    return summed.astype(jnp.bfloat16), gradients * weight_scale


def reference(hidden, out_grad, weights, momentum, block_cols, step_number):
    weight_scale = (4.0 / FF) ** 0.5

    def per_replica(items):
        return replica_pass(items[0], items[1], items[2], block_cols, weight_scale)

    outputs, gradients = lax.map(per_replica, (hidden.reshape(N_REPLICA, TOK, FF), out_grad.reshape(N_REPLICA, TOK, D), weights))
    level_count = N_REPLICA.bit_length() - 1
    chosen_bit = step_number[0] % level_count
    position = jnp.arange(N_REPLICA, dtype=jnp.int32)
    partner = jnp.bitwise_xor(position, jnp.left_shift(jnp.ones((), jnp.int32), chosen_bit.astype(jnp.int32)))
    own_w = weights.astype(jnp.float32)
    own_m = momentum.astype(jnp.float32)
    mate_w = weights[partner].astype(jnp.float32)
    mate_m = momentum[partner].astype(jnp.float32)
    mean_w = 0.5 * (own_w + mate_w)
    mean_m = 0.5 * (own_m + mate_m)
    corrected = gradients + LAMBDA_DC * gradients * gradients * (mean_w - own_w)
    moment_new = MOMENT_DECAY * mean_m + corrected
    weight_new = mean_w - LEARN_RATE * moment_new
    return outputs.reshape(TOKENS, D), weight_new.astype(jnp.bfloat16), moment_new.astype(jnp.bfloat16)
```

```python
import functools

import jax
import jax.numpy as jnp
from jax import lax
from jax.experimental import pallas as pl
from jax.experimental.pallas import tpu as pltpu
from jax.sharding import PartitionSpec as P

LAMBDA_DC = 1.0
MOMENT_DECAY = 0.9
LEARN_RATE = 0.2
VMEM_LIMIT = 32 * 1024 * 1024


def forward_kernel(scale, shards, me_ref, cols_ref, hid_ref, w_ref, *refs):
    slots, total = refs[:shards], refs[shards]
    step = pl.program_id(0)
    rows_step, block_size = w_ref.shape[0], w_ref.shape[1]
    per_row = w_ref.shape[2] // block_size

    @pl.when(step == 0)
    def _():
        total[...] = jnp.zeros_like(total)

    for i in range(rows_step):
        product = jnp.dot(
            hid_ref[:, i * block_size : (i + 1) * block_size],
            w_ref[i],
            preferred_element_type=jnp.float32,
        )
        for k in range(per_row):
            col = cols_ref[step * rows_step + i, k]
            total[col] += product[:, k * block_size : (k + 1) * block_size]

    @pl.when(step == pl.num_programs(0) - 1)
    def _():
        count = slots[0].shape[0]
        for s in range(shards):
            start = pl.multiple_of(lax.rem(me_ref[0] + s, shards) * count, count)
            for col in range(total.shape[0]):
                piece = total[col, pl.ds(start, count), :] * scale
                slots[s][:, col * block_size : (col + 1) * block_size] = piece.astype(jnp.bfloat16)


def forward_parts(me, cols, hidden, weights, scale, shards, model_width):
    tokens = hidden.shape[0]
    row_blocks, block_size, width = weights.shape
    rows_step = 2 if row_blocks % 2 == 0 else 1
    count = tokens // shards
    return pl.pallas_call(
        functools.partial(forward_kernel, scale, shards),
        out_shape=[jax.ShapeDtypeStruct((count, model_width), jnp.bfloat16)] * shards,
        grid_spec=pltpu.PrefetchScalarGridSpec(
            num_scalar_prefetch=2,
            grid=(row_blocks // rows_step,),
            in_specs=[
                pl.BlockSpec((tokens, rows_step * block_size), lambda r, *_: (0, r)),
                pl.BlockSpec((rows_step, block_size, width), lambda r, *_: (r, 0, 0)),
            ],
            out_specs=[pl.BlockSpec((count, model_width), lambda r, *_: (0, 0))] * shards,
            scratch_shapes=[pltpu.VMEM((model_width // block_size, tokens, block_size), jnp.float32)],
        ),
        compiler_params=pltpu.CompilerParams(vmem_limit_bytes=VMEM_LIMIT),
        cost_estimate=pl.CostEstimate(
            flops=2 * tokens * row_blocks * block_size * width,
            bytes_accessed=2 * (weights.size + hidden.size + tokens * model_width),
            transcendentals=0,
        ),
        name="forward_parts",
    )(me, cols, hidden, weights)


def update_kernel(scale, shards, me_ref, cols_ref, hid_ref, w_ref, m_ref, mate_w_ref, mate_m_ref, *refs):
    own, others = refs[0], refs[1 : 2 * shards - 1]
    new_w_ref, new_m_ref, section, sem = refs[2 * shards - 1 :]
    step = pl.program_id(0)
    rows_step, block_size = w_ref.shape[0], w_ref.shape[1]
    per_row = w_ref.shape[2] // block_size
    me = me_ref[0]
    count = own.shape[0]

    def copy_in(source, shard, number):
        start = pl.multiple_of(shard * count, count)
        return pltpu.make_async_copy(source, section.at[pl.ds(start, count), :], sem.at[number])

    def for_each(act):
        act(copy_in(own, me, 0))
        for s in range(1, shards):

            @pl.when(me >= s)
            def _(s=s):
                act(copy_in(others[2 * s - 2], me - s, 2 * s - 1))

            @pl.when(me + s < shards)
            def _(s=s):
                act(copy_in(others[2 * s - 1], me + s, 2 * s))

    @pl.when(step == 0)
    def _():
        for_each(lambda c: c.start())
        for_each(lambda c: c.wait())

    for i in range(rows_step):
        hid = hid_ref[:, i * block_size : (i + 1) * block_size]
        for k in range(per_row):
            col = cols_ref[step * rows_step + i, k]
            selected = section[:, pl.ds(pl.multiple_of(col * block_size, block_size), block_size)]
            gradient = scale * lax.dot_general(
                hid, selected, (((0,), (0,)), ((), ())), preferred_element_type=jnp.float32
            )
            at = (i, slice(None), slice(k * block_size, (k + 1) * block_size))
            own_w = w_ref[at].astype(jnp.float32)
            mean_w = 0.5 * (own_w + mate_w_ref[at].astype(jnp.float32))
            mean_m = 0.5 * (m_ref[at].astype(jnp.float32) + mate_m_ref[at].astype(jnp.float32))
            corrected = gradient + LAMBDA_DC * gradient * gradient * (mean_w - own_w)
            moment = MOMENT_DECAY * mean_m + corrected
            new_m_ref[at] = moment.astype(jnp.bfloat16)
            new_w_ref[at] = (mean_w - LEARN_RATE * moment).astype(jnp.bfloat16)


def update(me, cols, hidden, weights, momentum, mate_w, mate_m, section, scale, shards):
    tokens = hidden.shape[0]
    row_blocks, block_size, width = weights.shape
    rows_step = 2 if row_blocks % 2 == 0 else 1
    model_width = section[0].shape[1]
    blocks = pl.BlockSpec((rows_step, block_size, width), lambda r, *_: (r, 0, 0))
    shape = jax.ShapeDtypeStruct(weights.shape, jnp.bfloat16)
    return pl.pallas_call(
        functools.partial(update_kernel, scale, shards),
        out_shape=[shape, shape],
        grid_spec=pltpu.PrefetchScalarGridSpec(
            num_scalar_prefetch=2,
            grid=(row_blocks // rows_step,),
            in_specs=[pl.BlockSpec((tokens, rows_step * block_size), lambda r, *_: (0, r))]
            + [blocks] * 4
            + [pl.BlockSpec(memory_space=pl.ANY)] * len(section),
            out_specs=[blocks, blocks],
            scratch_shapes=[
                pltpu.VMEM((tokens, model_width), jnp.bfloat16),
                pltpu.SemaphoreType.DMA((2 * shards - 1,)),
            ],
        ),
        compiler_params=pltpu.CompilerParams(vmem_limit_bytes=VMEM_LIMIT),
        cost_estimate=pl.CostEstimate(
            flops=2 * tokens * weights.size,
            bytes_accessed=2 * (6 * weights.size + hidden.size + tokens * model_width),
            transcendentals=0,
        ),
        name="update",
    )(me, cols, hidden, weights, momentum, mate_w, mate_m, *section)


def gather_chain(own, shards):
    arrived, up, down = [], own, own
    for s in range(1, shards):
        up = lax.ppermute(up, "tensor", [(i, i + 1) for i in range(s - 1, shards - 1)])
        down = lax.ppermute(down, "tensor", [(i, i - 1) for i in range(shards - s, 0, -1)])
        arrived += [up, down]
    return arrived


def scatter_chain(slots, shards):
    up = down = None
    for t in range(shards - 1):
        send_up, send_down = slots[shards - 1 - t], slots[t + 1]
        if t:
            send_up, send_down = send_up + up, send_down + down
        up = lax.ppermute(send_up, "tensor", [(i, i + 1) for i in range(t + 1)])
        down = lax.ppermute(send_down, "tensor", [(shards - 1 - i, shards - 2 - i) for i in range(t + 1)])
    total = slots[0].astype(jnp.float32) + up.astype(jnp.float32) + down.astype(jnp.float32)
    return total.astype(jnp.bfloat16)


def step_for(bit, hidden, out_grad, weights, momentum, cols):
    shards = lax.axis_size("tensor")
    replicas = lax.axis_size("replica")
    model_width = out_grad.shape[1]
    scale = (4.0 / (hidden.shape[1] * shards)) ** 0.5
    me = lax.axis_index("tensor").reshape(1).astype(jnp.int32)
    pairs = [(i, i ^ 1 << bit) for i in range(replicas)]
    mate_w = lax.ppermute(weights, "replica", pairs)
    mate_m = lax.ppermute(momentum, "replica", pairs)
    arrived = gather_chain(out_grad, shards)
    slots = forward_parts(me, cols, hidden, weights, scale, shards, model_width)
    outputs = scatter_chain(slots, shards)
    new_w, new_m = update(
        me, cols, hidden, weights, momentum, mate_w, mate_m, [out_grad, *arrived], scale, shards
    )
    return outputs, new_w, new_m


def body(hidden, out_grad, weights, momentum, block_cols, step_number):
    levels = lax.axis_size("replica").bit_length() - 1
    outputs, new_w, new_m = lax.switch(
        lax.rem(step_number[0], levels),
        [functools.partial(step_for, bit) for bit in range(levels)],
        hidden,
        out_grad,
        weights[0],
        momentum[0],
        block_cols,
    )
    return outputs, new_w[None], new_m[None]


def solution(mesh):
    return jax.shard_map(
        body,
        mesh=mesh,
        in_specs=(
            P("replica", "tensor"),
            P(("replica", "tensor"), None),
            P("replica", "tensor", None, None),
            P("replica", "tensor", None, None),
            P("tensor", None),
            P(),
        ),
        out_specs=(
            P(("replica", "tensor"), None),
            P("replica", "tensor", None, None),
            P("replica", "tensor", None, None),
        ),
        check_vma=False,
    )
```

```python
import functools

import jax
import jax.numpy as jnp
from jax import lax
from jax.experimental import pallas as pl
from jax.experimental.pallas import tpu as pltpu
from jax.sharding import PartitionSpec as P

LAMBDA_DC = 1.0
MOMENT_DECAY = 0.9
LEARN_RATE = 0.2
VMEM_LIMIT = 14 * 1024 * 1024
LIGHT = pl.CostEstimate(flops=1024, bytes_accessed=1024, transcendentals=0)
ANYWHERE = pl.BlockSpec(memory_space=pl.ANY)
IN_VMEM = pl.BlockSpec(memory_space=pltpu.VMEM)


def rows_per_step(row_blocks):
    return 2 if row_blocks % 2 == 0 else 1


def forward_kernel(scale, shards, pieces, me_ref, cols_ref, hid_ref, w_ref, *refs):
    parts, total = refs[:-1], refs[-1]
    step = pl.program_id(0)
    rows_step, block_size = w_ref.shape[0], w_ref.shape[1]
    per_row = w_ref.shape[2] // block_size

    @pl.when(step == 0)
    def _():
        total[...] = jnp.zeros_like(total)

    for i in range(rows_step):
        product = jnp.dot(
            hid_ref[:, i * block_size : (i + 1) * block_size],
            w_ref[i],
            preferred_element_type=jnp.float32,
        )
        for k in range(per_row):
            col = cols_ref[k, step * rows_step + i]
            total[col] += product[:, k * block_size : (k + 1) * block_size]

    @pl.when(step == pl.num_programs(0) - 1)
    def _():
        me = me_ref[0]
        even = lax.rem(me, 2) == 0
        below, above = jnp.where(even, me, shards - 1 - me), jnp.where(even, shards - 1 - me, me)
        ahead = jnp.where(even, 1, -1)
        kept = [(me, None)]
        for p in range(1, shards):
            kept += [(me + ahead * (shards - p), below <= p - 1), (me - ahead * (shards - p), above <= p - 1)]
        rows = parts[0].shape[0]
        for number, part in enumerate(parts):
            owner, used = kept[number // pieces]
            factor = scale if used is None else jnp.where(used, scale, 0.0)
            place = jnp.clip(owner, 0, shards - 1) * pieces + number % pieces
            start = pl.multiple_of(place * rows, rows)
            for col in range(total.shape[0]):
                value = total[col, pl.ds(start, rows), :] * factor
                part[:, col * block_size : (col + 1) * block_size] = value.astype(jnp.bfloat16)


def forward_parts(me, cols, hidden, weights, scale, shards, pieces, model_width):
    tokens = hidden.shape[0]
    row_blocks, block_size, width = weights.shape
    rows_step = rows_per_step(row_blocks)
    rows = tokens // shards // pieces
    count = pieces * (2 * shards - 1)
    return pl.pallas_call(
        functools.partial(forward_kernel, scale, shards, pieces),
        out_shape=[jax.ShapeDtypeStruct((rows, model_width), jnp.bfloat16)] * count,
        grid_spec=pltpu.PrefetchScalarGridSpec(
            num_scalar_prefetch=2,
            grid=(row_blocks // rows_step,),
            in_specs=[
                pl.BlockSpec((tokens, rows_step * block_size), lambda r, *_: (0, r)),
                pl.BlockSpec((rows_step, block_size, width), lambda r, *_: (r, 0, 0)),
            ],
            out_specs=[pl.BlockSpec((rows, model_width), lambda r, *_: (0, 0))] * count,
            scratch_shapes=[pltpu.VMEM((model_width // block_size, tokens, block_size), jnp.float32)],
        ),
        compiler_params=pltpu.CompilerParams(vmem_limit_bytes=VMEM_LIMIT),
        cost_estimate=LIGHT,
        name="forward_parts",
    )(me, cols, hidden, weights)


def put_shards(me, shards, given, section, sem):
    ahead = 1 - 2 * lax.rem(me, 2)
    for act in ("start", "wait"):
        for number, (step, side, piece, pieces, ref) in enumerate(given):
            shard = me + ahead * (step if side == 0 else -step)
            rows = ref.shape[0]

            @pl.when((shard >= 0) & (shard < shards))
            def _(act=act, number=number, piece=piece, pieces=pieces, ref=ref, shard=shard, rows=rows):
                to = section.at[pl.ds(pl.multiple_of((shard * pieces + piece) * rows, rows), rows), :]
                getattr(pltpu.make_async_copy(ref, to, sem.at[number]), act)()


def section_kernel(shards, labels, me_ref, *refs):
    section, sem = refs[-2:]
    put_shards(me_ref[0], shards, [(*a, r) for a, r in zip(labels, refs)], section, sem)


def start_section(me, shards, given):
    labels, arrays = [a for a, _ in given], [a for _, a in given]
    rows, width = arrays[0].shape
    return pl.pallas_call(
        functools.partial(section_kernel, shards, labels),
        out_shape=jax.ShapeDtypeStruct((rows * labels[0][3] * shards, width), jnp.bfloat16),
        grid_spec=pltpu.PrefetchScalarGridSpec(
            num_scalar_prefetch=1,
            grid=(),
            in_specs=[ANYWHERE] * len(arrays),
            out_specs=IN_VMEM,
            scratch_shapes=[pltpu.SemaphoreType.DMA((len(arrays),))],
        ),
        compiler_params=pltpu.CompilerParams(vmem_limit_bytes=VMEM_LIMIT),
        cost_estimate=LIGHT,
        name="start_section",
    )(me, *arrays)


def update_kernel(scale, shards, first, count, labels, me_ref, cols_ref, hid_ref, w_ref, m_ref, mate_w_ref, mate_m_ref, section, *refs):
    late, (held_w, held_m, sem) = refs[: len(labels)], refs[-3:]
    new_w_ref, new_m_ref = refs[-6:-4] if labels else refs[-5:-3]
    block_size = w_ref.shape[1]
    per_row = w_ref.shape[2] // block_size
    if labels:
        section = refs[-4]
        put_shards(me_ref[0], shards, [(*a, r) for a, r in zip(labels, late)], section, sem.at[2])

    def copies_out(i):
        return [
            pltpu.make_async_copy(held.at[i], new.at[first + i], sem.at[number, i])
            for number, (held, new) in enumerate(((held_w, new_w_ref), (held_m, new_m_ref)))
        ]

    for i in range(count):
        hid = hid_ref[:, i * block_size : (i + 1) * block_size].T
        for k in range(0, per_row, 2):
            selected = []
            for j in range(2):
                col = cols_ref[k + j, first + i]
                selected.append(section[:, pl.ds(pl.multiple_of(col * block_size, block_size), block_size)])
            gradient = scale * jnp.dot(hid, jnp.concatenate(selected, 1), preferred_element_type=jnp.float32)
            at = (slice(None), slice(k * block_size, (k + 2) * block_size))
            own_w, mate_w = w_ref[i, *at], mate_w_ref[i, *at]
            half_gap = 0.5 * (mate_w - own_w).astype(jnp.float32)
            mean_w = 0.5 * (own_w + mate_w).astype(jnp.float32)
            corrected = gradient + LAMBDA_DC * gradient * gradient * half_gap
            moment = (0.5 * MOMENT_DECAY) * (m_ref[i, *at] + mate_m_ref[i, *at]).astype(jnp.float32) + corrected
            held_m[i, *at] = moment.astype(jnp.bfloat16)
            held_w[i, *at] = (mean_w - LEARN_RATE * moment).astype(jnp.bfloat16)
        for copy in copies_out(i):
            copy.start()
    for i in range(count):
        for copy in copies_out(i):
            copy.wait()


def update(me, cols, hidden, weights, momentum, mate_w, mate_m, section, late, scale, shards, first, made):
    count, block_size, width = mate_w.shape
    shape = jax.ShapeDtypeStruct(weights.shape, jnp.bfloat16)
    labels, arrays = [a for a, _ in late], [a for _, a in late]
    aliases = {8 + len(arrays) + i: i for i in range(len(made))}
    if late:
        aliases[7] = 2
    held = pltpu.VMEM((count, block_size, width), jnp.bfloat16)
    window = pl.BlockSpec((count, block_size, width), lambda i, *_: (first // count, 0, 0))
    whole = pl.BlockSpec(mate_w.shape, lambda i, *_: (0, 0, 0))
    hid = pl.BlockSpec((hidden.shape[0], count * block_size), lambda i, *_: (0, first // count))
    new = pl.pallas_call(
        functools.partial(update_kernel, scale, shards, first, count, labels),
        out_shape=[shape, shape] + [jax.ShapeDtypeStruct(section.shape, section.dtype)] * bool(late),
        grid_spec=pltpu.PrefetchScalarGridSpec(
            num_scalar_prefetch=2,
            grid=(1,),
            in_specs=[hid, window, window, whole, window, IN_VMEM] + [ANYWHERE] * (len(arrays) + len(made)),
            out_specs=[ANYWHERE, ANYWHERE] + [IN_VMEM] * bool(late),
            scratch_shapes=[held, held, pltpu.SemaphoreType.DMA((3, max(count, len(arrays))))],
        ),
        input_output_aliases=aliases,
        compiler_params=pltpu.CompilerParams(vmem_limit_bytes=VMEM_LIMIT),
        cost_estimate=LIGHT,
        name="update",
    )(me, cols, hidden, weights, momentum, mate_w, mate_m, section, *arrays, *made)
    return new[:2]


def add_kernel(*refs):
    (*terms, total, held, sem) = refs
    rows = terms[0].shape[0]
    for h in range(len(terms) // 3):
        for r in range(0, rows, 16):
            values = [t[r : r + 16, :].astype(jnp.float32) for t in terms[3 * h : 3 * h + 3]]
            held[h * rows + r : h * rows + r + 16, :] = sum(values).astype(jnp.bfloat16)
    copy = pltpu.make_async_copy(held, total, sem)
    copy.start()
    copy.wait()


def add_up(pieces):
    rows, width = pieces[0][0].shape
    shape = (rows * len(pieces), width)
    return pl.pallas_call(
        add_kernel,
        out_shape=jax.ShapeDtypeStruct(shape, jnp.bfloat16),
        in_specs=[IN_VMEM] * (3 * len(pieces)),
        out_specs=pl.BlockSpec(memory_space=pltpu.HBM),
        scratch_shapes=[pltpu.VMEM(shape, jnp.bfloat16), pltpu.SemaphoreType.DMA],
        compiler_params=pltpu.CompilerParams(vmem_limit_bytes=VMEM_LIMIT),
        cost_estimate=LIGHT,
        name="add_up",
    )(*[a for piece in pieces for a in piece])


def exchange(value, parity, shards):
    pairs = [(i, i + 1) for i in range(parity, shards - 1, 2)]
    return lax.ppermute(value, "tensor", pairs + [(j, i) for i, j in pairs])


def gather_and_scatter(own, make_parts, after_phase, along, shards, pieces):
    rows = own.shape[0] // pieces
    given, got = [((0, 0, 0, 1), own)], []
    for h in range(pieces):
        piece = own[h * rows : (h + 1) * rows]
        got.append([exchange(piece, side, shards) for side in (0, 1)])
    parts = make_parts()
    for p in range(1, shards):
        for h in range(pieces):
            got[h], parts, along[p - 1] = lax.optimization_barrier((got[h], parts, along[p - 1]))
            given += [((p, side, h, pieces), got[h][side]) for side in (0, 1)]
            part = [parts[(2 * p - 1 + side) * pieces + h] for side in (0, 1)]
            got[h] = [exchange(got[h][1 - side] + part[side], side, shards) for side in (0, 1)]
        if p == shards - 1 and pieces > 1:
            label, last = given[-1]
            last, got[:-1] = lax.optimization_barrier((last, got[:-1]))
            given[-1] = (label, last)
        result = after_phase(p, given, parts)
    result, along[shards - 1], got = lax.optimization_barrier((result, along[shards - 1], got))
    return result, add_up([(parts[h], *got[h]) for h in range(pieces)])


def step_for(bit, hidden, out_grad, weights, momentum, block_cols):
    shards = lax.axis_size("tensor")
    replicas = lax.axis_size("replica")
    model_width = out_grad.shape[1]
    scale = (4.0 / (hidden.shape[1] * shards)) ** 0.5
    me = lax.axis_index("tensor").reshape(1).astype(jnp.int32)
    cols = block_cols.T
    row_blocks = weights.shape[0]
    fixed = (me, cols, hidden, weights, momentum)

    def swap(value):
        return lax.ppermute(value, "replica", [(i, i ^ 1 << bit) for i in range(replicas)])

    def forward(pieces):
        return lambda: forward_parts(me, cols, hidden, weights, scale, shards, pieces, model_width)

    along = [[] for _ in range(shards)]
    along[0].append(swap(momentum))
    if bit == 0:
        counted = []

        def beside(p, given, parts):
            if p == 1:
                behind, _ = lax.optimization_barrier((weights, parts[0]))
                along[1].append(swap(behind))
            if p == shards - 2:
                counted.append(len(given))
                along[p].append(start_section(me, shards, given))
            if p == shards - 1:
                (mate_m,), (mate_w,) = along[:2]
                (section,), (count,) = along[p - 1], counted
                return update(*fixed, mate_w, mate_m, section, given[count:], scale, shards, 0, [])

        made, outputs = gather_and_scatter(out_grad, forward(2), beside, along, shards, 2)
        return outputs, *made

    cut = row_blocks - rows_per_step(row_blocks)
    head, tail = swap(weights[:cut]), swap(weights[cut:])

    def gathered(p, given, parts):
        return start_section(me, shards, given) if p == shards - 1 else None

    section, outputs = gather_and_scatter(out_grad, forward(1), gathered, along, shards, 1)
    ((mate_m,), *_) = along
    head, outputs = lax.optimization_barrier((head, outputs))
    made = update(*fixed, head, mate_m, section, [], scale, shards, 0, [])
    made = update(*fixed, tail, mate_m, section, [], scale, shards, cut, made)
    return outputs, *made


def body(hidden, out_grad, weights, momentum, block_cols, step_number):
    levels = lax.axis_size("replica").bit_length() - 1
    outputs, new_w, new_m = lax.switch(
        lax.rem(step_number[0], levels),
        [functools.partial(step_for, bit) for bit in range(levels)],
        hidden,
        out_grad,
        weights[0],
        momentum[0],
        block_cols,
    )
    return outputs, new_w[None], new_m[None]


def solution(mesh):
    return jax.shard_map(
        body,
        mesh=mesh,
        in_specs=(
            P("replica", "tensor"),
            P(("replica", "tensor"), None),
            P("replica", "tensor", None, None),
            P("replica", "tensor", None, None),
            P("tensor", None),
            P(),
        ),
        out_specs=(
            P(("replica", "tensor"), None),
            P("replica", "tensor", None, None),
            P("replica", "tensor", None, None),
        ),
        check_vma=False,
    )
```

```python
import functools

import jax
import jax.numpy as jnp
from jax import lax
from jax.experimental import pallas as pl
from jax.experimental.pallas import tpu as pltpu
from jax.sharding import PartitionSpec as P

LAMBDA_DC = 1.0
MOMENT_DECAY = 0.9
LEARN_RATE = 0.2
MIB = 1024 * 1024
LIGHT = pl.CostEstimate(flops=1024, bytes_accessed=1024, transcendentals=0)
ANYWHERE = pl.BlockSpec(memory_space=pl.ANY)
IN_VMEM = pl.BlockSpec(memory_space=pltpu.VMEM)


def rows_per_step(row_blocks):
    return 2 if row_blocks % 2 == 0 else 1


def forward_kernel(scale, shards, pieces, me_ref, cols_ref, hid_ref, w_ref, *refs):
    parts, total = refs[:-1], refs[-1]
    step = pl.program_id(0)
    rows_step, block_size = w_ref.shape[0], w_ref.shape[1]
    per_row = w_ref.shape[2] // block_size

    @pl.when(step == 0)
    def _():
        total[...] = jnp.zeros_like(total)

    for i in range(rows_step):
        product = jnp.dot(
            hid_ref[:, i * block_size : (i + 1) * block_size],
            w_ref[i],
            preferred_element_type=jnp.float32,
        )
        for k in range(per_row):
            col = cols_ref[k, step * rows_step + i]
            total[col] += product[:, k * block_size : (k + 1) * block_size]

    @pl.when(step == pl.num_programs(0) - 1)
    def _():
        me = me_ref[0]
        even = lax.rem(me, 2) == 0
        below, above = jnp.where(even, me, shards - 1 - me), jnp.where(even, shards - 1 - me, me)
        ahead = jnp.where(even, 1, -1)
        kept = [(me, None)]
        for p in range(1, shards):
            kept += [(me + ahead * (shards - p), below <= p - 1), (me - ahead * (shards - p), above <= p - 1)]
        rows = parts[0].shape[0]
        ends = []
        for number, part in enumerate(parts):
            owner, used = kept[number // pieces]
            factor = scale if used is None else jnp.where(used, scale, 0.0)
            place = jnp.clip(owner, 0, shards - 1) * pieces + number % pieces
            start = pl.multiple_of(place * rows, rows)
            ends.append((part, start, factor))

        def finish(col, _):
            to = pl.ds(pl.multiple_of(col * block_size, block_size), block_size)
            for part, start, factor in ends:
                part[:, to] = (total[col, pl.ds(start, rows), :] * factor).astype(jnp.bfloat16)
            return 0

        lax.fori_loop(0, total.shape[0], finish, 0)


def forward_parts(me, cols, hidden, weights, scale, shards, pieces, model_width):
    tokens = hidden.shape[0]
    row_blocks, block_size, width = weights.shape
    rows_step = rows_per_step(row_blocks)
    rows = tokens // shards // pieces
    count = pieces * (2 * shards - 1)
    return pl.pallas_call(
        functools.partial(forward_kernel, scale, shards, pieces),
        out_shape=[jax.ShapeDtypeStruct((rows, model_width), jnp.bfloat16)] * count,
        grid_spec=pltpu.PrefetchScalarGridSpec(
            num_scalar_prefetch=2,
            grid=(row_blocks // rows_step,),
            in_specs=[
                pl.BlockSpec((tokens, rows_step * block_size), lambda r, *_: (0, r)),
                pl.BlockSpec((rows_step, block_size, width), lambda r, *_: (r, 0, 0)),
            ],
            out_specs=[IN_VMEM] * count,
            scratch_shapes=[pltpu.VMEM((model_width // block_size, tokens, block_size), jnp.float32)],
        ),
        compiler_params=pltpu.CompilerParams(vmem_limit_bytes=10 * MIB),
        cost_estimate=LIGHT,
        name="forward_parts",
    )(me, cols, hidden, weights)


def put_shards(me, shards, given, section, sem):
    ahead = 1 - 2 * lax.rem(me, 2)
    for act in ("start", "wait"):
        for number, (step, side, piece, pieces, ref) in enumerate(given):
            shard = me + ahead * (step if side == 0 else -step)
            rows = ref.shape[0]

            @pl.when((shard >= 0) & (shard < shards))
            def _(act=act, number=number, piece=piece, pieces=pieces, ref=ref, shard=shard, rows=rows):
                to = section.at[pl.ds(pl.multiple_of((shard * pieces + piece) * rows, rows), rows), :]
                getattr(pltpu.make_async_copy(ref, to, sem.at[number]), act)()


def section_kernel(shards, labels, me_ref, *refs):
    *given, whole, section, staged, sem = refs
    copy = pltpu.make_async_copy(whole, staged, sem.at[len(given)])
    copy.start()
    put_shards(me_ref[0], shards, [(*a, r) for a, r in zip(labels, given)], section, sem)
    copy.wait()


def start_section(me, shards, given, whole):
    labels, arrays = [a for a, _ in given], [a for _, a in given]
    rows, width = arrays[0].shape
    return pl.pallas_call(
        functools.partial(section_kernel, shards, labels),
        out_shape=[
            jax.ShapeDtypeStruct((rows * labels[0][3] * shards, width), jnp.bfloat16),
            jax.ShapeDtypeStruct(whole.shape, whole.dtype),
        ],
        grid_spec=pltpu.PrefetchScalarGridSpec(
            num_scalar_prefetch=1,
            grid=(),
            in_specs=[ANYWHERE] * (len(arrays) + 1),
            out_specs=[IN_VMEM, IN_VMEM],
            scratch_shapes=[pltpu.SemaphoreType.DMA((len(arrays) + 1,))],
        ),
        compiler_params=pltpu.CompilerParams(vmem_limit_bytes=4 * MIB),
        cost_estimate=LIGHT,
        name="start_section",
    )(me, *arrays, whole)


def update_kernel(scale, shards, first, count, labels, me_ref, cols_ref, hid_ref, w_ref, m_ref, mate_w_ref, mate_m_ref, section, *refs):
    late, (held_w, held_m, sem) = refs[: len(labels)], refs[-3:]
    new_w_ref, new_m_ref = refs[-6:-4] if labels else refs[-5:-3]
    block_size = w_ref.shape[1]
    per_row = w_ref.shape[2] // block_size
    if labels:
        section = refs[-4]
        put_shards(me_ref[0], shards, [(*a, r) for a, r in zip(labels, late)], section, sem.at[2])

    def copies_out(i):
        return [
            pltpu.make_async_copy(held.at[i], new.at[first + i], sem.at[number, i])
            for number, (held, new) in enumerate(((held_w, new_w_ref), (held_m, new_m_ref)))
        ]

    for i in range(count):
        hid = hid_ref[:, i * block_size : (i + 1) * block_size].T
        for k in range(0, per_row, 2):
            selected = []
            for j in range(2):
                col = cols_ref[k + j, first + i]
                selected.append(section[:, pl.ds(pl.multiple_of(col * block_size, block_size), block_size)])
            gradient = scale * jnp.dot(hid, jnp.concatenate(selected, 1), preferred_element_type=jnp.float32)
            at = (slice(None), slice(k * block_size, (k + 2) * block_size))
            own_w, mate_w = w_ref[i, *at], mate_w_ref[i, *at]
            half_gap = 0.5 * (mate_w - own_w).astype(jnp.float32)
            mean_w = 0.5 * (own_w + mate_w).astype(jnp.float32)
            corrected = gradient + LAMBDA_DC * gradient * gradient * half_gap
            moment = (0.5 * MOMENT_DECAY) * (m_ref[i, *at] + mate_m_ref[i, *at]).astype(jnp.float32) + corrected
            held_m[i, *at] = moment.astype(jnp.bfloat16)
            held_w[i, *at] = (mean_w - LEARN_RATE * moment).astype(jnp.bfloat16)
        for copy in copies_out(i):
            copy.start()
    for i in range(count):
        for copy in copies_out(i):
            copy.wait()


def update(me, cols, hidden, weights, momentum, mate_w, mate_m, section, late, scale, shards, first, count, made):
    block_size, width = mate_w.shape[1:]
    mate_first = first if mate_w.shape[0] == weights.shape[0] else 0
    shape = jax.ShapeDtypeStruct(weights.shape, jnp.bfloat16)
    labels, arrays = [a for a, _ in late], [a for _, a in late]
    aliases = {8 + len(arrays) + i: i for i in range(len(made))}
    if late:
        aliases[7] = 2
    held = pltpu.VMEM((count, block_size, width), jnp.bfloat16)
    window = pl.BlockSpec((count, block_size, width), lambda i, *_: (first // count, 0, 0))
    mates = pl.BlockSpec((count, block_size, width), lambda i, *_: (mate_first // count, 0, 0))
    hid = pl.BlockSpec((hidden.shape[0], count * block_size), lambda i, *_: (0, first // count))
    new = pl.pallas_call(
        functools.partial(update_kernel, scale, shards, first, count, labels),
        out_shape=[shape, shape] + [jax.ShapeDtypeStruct(section.shape, section.dtype)] * bool(late),
        grid_spec=pltpu.PrefetchScalarGridSpec(
            num_scalar_prefetch=2,
            grid=(1,),
            in_specs=[hid, window, window, mates, window, IN_VMEM] + [ANYWHERE] * (len(arrays) + len(made)),
            out_specs=[ANYWHERE, ANYWHERE] + [IN_VMEM] * bool(late),
            scratch_shapes=[held, held, pltpu.SemaphoreType.DMA((3, max(count, len(arrays))))],
        ),
        input_output_aliases=aliases,
        compiler_params=pltpu.CompilerParams(vmem_limit_bytes=16 * MIB),
        cost_estimate=LIGHT,
        name="update",
    )(me, cols, hidden, weights, momentum, mate_w, mate_m, section, *arrays, *made)
    return list(new)


def add_kernel(*refs):
    (*done, own, got_a, got_b, total, held, sem) = refs
    rows = own.shape[0]
    copies = [
        pltpu.make_async_copy(ref, total.at[pl.ds(h * rows, rows)], sem.at[h]) for h, ref in enumerate((*done, held))
    ]
    for copy in copies[:-1]:
        copy.start()
    for r in range(0, rows, 16):
        at = slice(r, r + 16)
        held[at, :] = sum(t[at, :].astype(jnp.float32) for t in (own, got_a, got_b)).astype(jnp.bfloat16)
    copies[-1].start()
    for copy in copies:
        copy.wait()


def add_up(done, terms):
    rows, width = terms[0].shape
    count = len(done) + 1
    return pl.pallas_call(
        add_kernel,
        out_shape=jax.ShapeDtypeStruct((rows * count, width), jnp.bfloat16),
        in_specs=[ANYWHERE] * len(done) + [IN_VMEM] * 3,
        out_specs=pl.BlockSpec(memory_space=pltpu.HBM),
        scratch_shapes=[pltpu.VMEM((rows, width), jnp.bfloat16), pltpu.SemaphoreType.DMA((count,))],
        compiler_params=pltpu.CompilerParams(vmem_limit_bytes=4 * MIB),
        cost_estimate=LIGHT,
        name="add_up",
    )(*done, *terms)


def exchange(value, parity, shards):
    pairs = [(i, i + 1) for i in range(parity, shards - 1, 2)]
    return lax.ppermute(value, "tensor", pairs + [(j, i) for i, j in pairs])


def gather_and_scatter(own, make_parts, after_phase, along, shards, pieces):
    rows = own.shape[0] // pieces
    whole = [exchange(own, side, shards) for side in (0, 1)]
    parts = make_parts()
    whole, parts, along[0] = lax.optimization_barrier((whole, parts, along[0]))
    given = [((0, 0, 0, 1), own)] + [((1, side, 0, 1), whole[side]) for side in (0, 1)]
    got = [[a[h * rows : (h + 1) * rows] for a in whole] for h in range(pieces)]
    for p in range(1, shards):
        for h in range(pieces):
            if p > 1:
                got[h], parts, along[p - 1] = lax.optimization_barrier((got[h], parts, along[p - 1]))
                given += [((p, side, h, pieces), got[h][side]) for side in (0, 1)]
            part = [parts[(2 * p - 1 + side) * pieces + h] for side in (0, 1)]
            got[h] = [exchange(got[h][1 - side] + part[side], side, shards) for side in (0, 1)]
        result = after_phase(p, given, parts)
    totals = []
    for h in range(pieces):
        result, along[shards - 1], got[h] = lax.optimization_barrier((result, along[shards - 1], got[h]))
        if h < pieces - 1:
            totals.append(sum(a.astype(jnp.float32) for a in (parts[h], *got[h])).astype(jnp.bfloat16))
            result, totals = lax.optimization_barrier((result, totals))
    return result, add_up(totals, (parts[pieces - 1], *got[-1]))


def step_for(bit, hidden, out_grad, weights, momentum, block_cols):
    shards = lax.axis_size("tensor")
    replicas = lax.axis_size("replica")
    model_width = out_grad.shape[1]
    scale = (4.0 / (hidden.shape[1] * shards)) ** 0.5
    me = lax.axis_index("tensor").reshape(1).astype(jnp.int32)
    cols = block_cols.T
    row_blocks = weights.shape[0]
    fixed = (me, cols, hidden, weights, momentum)

    def swap(value):
        return lax.ppermute(value, "replica", [(i, i ^ 1 << bit) for i in range(replicas)])

    def forward(pieces):
        return lambda: forward_parts(me, cols, hidden, weights, scale, shards, pieces, model_width)

    along = [[] for _ in range(shards)]
    along[0].append(swap(momentum))
    if bit == 0:
        counted = []

        def beside(p, given, parts):
            if p == 1:
                behind, _ = lax.optimization_barrier((weights, parts[0]))
                along[shards - 2].append(swap(behind))
            if p == shards - 2:
                counted.append(len(given))
                along[p] += start_section(me, shards, given, along[0][0])
            if p == shards - 1:
                (count,), (mate_w, section, mate_m) = counted, along[shards - 2]
                late = given[count:]
                return update(*fixed, mate_w, mate_m, section, late, scale, shards, 0, row_blocks, [])[:2]

        made, outputs = gather_and_scatter(out_grad, forward(2), beside, along, shards, 2)
        return outputs, *made

    cut = row_blocks - rows_per_step(row_blocks)
    head, tail = swap(weights[:cut]), swap(weights[cut:])

    def gathered(p, given, parts):
        return start_section(me, shards, given, along[0][0]) if p == shards - 1 else None

    (section, mate_m), outputs = gather_and_scatter(out_grad, forward(1), gathered, along, shards, 1)
    head, outputs = lax.optimization_barrier((head, outputs))
    made = update(*fixed, head, mate_m, section, [], scale, shards, 0, cut, [])
    made = update(*fixed, tail, mate_m, section, [], scale, shards, cut, row_blocks - cut, made)
    return outputs, *made


def body(hidden, out_grad, weights, momentum, block_cols, step_number):
    levels = lax.axis_size("replica").bit_length() - 1
    outputs, new_w, new_m = lax.switch(
        lax.rem(step_number[0], levels),
        [functools.partial(step_for, bit) for bit in range(levels)],
        hidden,
        out_grad,
        weights[0],
        momentum[0],
        block_cols,
    )
    return outputs, new_w[None], new_m[None]


def solution(mesh):
    return jax.shard_map(
        body,
        mesh=mesh,
        in_specs=(
            P("replica", "tensor"),
            P(("replica", "tensor"), None),
            P("replica", "tensor", None, None),
            P("replica", "tensor", None, None),
            P("tensor", None),
            P(),
        ),
        out_specs=(
            P(("replica", "tensor"), None),
            P("replica", "tensor", None, None),
            P("replica", "tensor", None, None),
        ),
        check_vma=False,
    )
```

```python
import functools

import jax
import jax.numpy as jnp
from jax import lax
from jax.experimental import pallas as pl
from jax.experimental.pallas import tpu as pltpu
from jax.sharding import PartitionSpec as P

LAMBDA_DC = 1.0
MOMENT_DECAY = 0.9
LEARN_RATE = 0.2
MIB = 1024 * 1024
LIGHT = pl.CostEstimate(flops=1024, bytes_accessed=1024, transcendentals=0)
ANYWHERE = pl.BlockSpec(memory_space=pl.ANY)
IN_VMEM = pl.BlockSpec(memory_space=pltpu.VMEM)
IN_SMEM = pl.BlockSpec(memory_space=pltpu.SMEM)


def rows_per_step(row_blocks):
    return 2 if row_blocks % 2 == 0 else 1


def forward_kernel(scale, shards, pieces, me_ref, cols_ref, hid_ref, w_ref, *refs):
    parts, total = refs[:-1], refs[-1]
    step = pl.program_id(0)
    rows_step, block_size = w_ref.shape[0], w_ref.shape[1]
    per_row = w_ref.shape[2] // block_size

    @pl.when(step == 0)
    def _():
        total[...] = jnp.zeros_like(total)

    for i in range(rows_step):
        product = jnp.dot(
            hid_ref[:, i * block_size : (i + 1) * block_size],
            w_ref[i],
            preferred_element_type=jnp.float32,
        )
        for k in range(per_row):
            col = cols_ref[k, step * rows_step + i]
            total[col] += product[:, k * block_size : (k + 1) * block_size]

    @pl.when(step == pl.num_programs(0) - 1)
    def _():
        me = me_ref[0]
        even = lax.rem(me, 2) == 0
        below, above = jnp.where(even, me, shards - 1 - me), jnp.where(even, shards - 1 - me, me)
        ahead = jnp.where(even, 1, -1)
        kept = [(me, None)]
        for p in range(1, shards):
            kept += [(me + ahead * (shards - p), below <= p - 1), (me - ahead * (shards - p), above <= p - 1)]
        rows = parts[0].shape[0]
        ends = []
        for number, part in enumerate(parts):
            owner, used = kept[number // pieces]
            factor = scale if used is None else jnp.where(used, scale, 0.0)
            place = jnp.clip(owner, 0, shards - 1) * pieces + number % pieces
            start = pl.multiple_of(place * rows, rows)
            ends.append((part, start, factor))

        def finish(col, _):
            to = pl.ds(pl.multiple_of(col * block_size, block_size), block_size)
            for part, start, factor in ends:
                part[:, to] = (total[col, pl.ds(start, rows), :] * factor).astype(jnp.bfloat16)
            return 0

        lax.fori_loop(0, total.shape[0], finish, 0)


def forward_parts(me, cols, hidden, weights, scale, shards, pieces, model_width):
    tokens = hidden.shape[0]
    row_blocks, block_size, width = weights.shape
    rows_step = rows_per_step(row_blocks)
    rows = tokens // shards // pieces
    count = pieces * (2 * shards - 1)
    return pl.pallas_call(
        functools.partial(forward_kernel, scale, shards, pieces),
        out_shape=[jax.ShapeDtypeStruct((rows, model_width), jnp.bfloat16)] * count,
        grid=(row_blocks // rows_step,),
        in_specs=[
            IN_SMEM,
            IN_SMEM,
            pl.BlockSpec((tokens, rows_step * block_size), lambda r: (0, r)),
            pl.BlockSpec((rows_step, block_size, width), lambda r: (r, 0, 0)),
        ],
        out_specs=[IN_VMEM] * count,
        scratch_shapes=[pltpu.VMEM((model_width // block_size, tokens, block_size), jnp.float32)],
        compiler_params=pltpu.CompilerParams(vmem_limit_bytes=10 * MIB),
        cost_estimate=LIGHT,
        name="forward_parts",
    )(me, cols, hidden, weights)


def put_shards(me, shards, given, section, sem):
    ahead = 1 - 2 * lax.rem(me, 2)
    for act in ("start", "wait"):
        for number, (step, side, piece, pieces, ref) in enumerate(given):
            shard = me + ahead * (step if side == 0 else -step)
            rows = ref.shape[0]

            @pl.when((shard >= 0) & (shard < shards))
            def _(act=act, number=number, piece=piece, pieces=pieces, ref=ref, shard=shard, rows=rows):
                to = section.at[pl.ds(pl.multiple_of((shard * pieces + piece) * rows, rows), rows), :]
                getattr(pltpu.make_async_copy(ref, to, sem.at[number]), act)()


def section_kernel(shards, labels, me_ref, *refs):
    *given, whole, section, staged, sem = refs
    copy = pltpu.make_async_copy(whole, staged, sem.at[len(given)])
    copy.start()
    put_shards(me_ref[0], shards, [(*a, r) for a, r in zip(labels, given)], section, sem)
    copy.wait()


def start_section(me, shards, given, whole):
    labels, arrays = [a for a, _ in given], [a for _, a in given]
    rows, width = arrays[0].shape
    return pl.pallas_call(
        functools.partial(section_kernel, shards, labels),
        out_shape=[
            jax.ShapeDtypeStruct((rows * labels[0][3] * shards, width), jnp.bfloat16),
            jax.ShapeDtypeStruct(whole.shape, whole.dtype),
        ],
        grid=(),
        in_specs=[IN_SMEM] + [ANYWHERE] * (len(arrays) + 1),
        out_specs=[IN_VMEM, IN_VMEM],
        scratch_shapes=[pltpu.SemaphoreType.DMA((len(arrays) + 1,))],
        compiler_params=pltpu.CompilerParams(vmem_limit_bytes=4 * MIB),
        cost_estimate=LIGHT,
        name="start_section",
    )(me, *arrays, whole)


def update_kernel(scale, shards, first, count, labels, me_ref, cols_ref, hid_ref, w_ref, m_ref, mate_w_ref, mate_m_ref, section, *refs):
    late, (held_w, held_m, sem) = refs[: len(labels)], refs[-3:]
    new_w_ref, new_m_ref = refs[-6:-4] if labels else refs[-5:-3]
    block_size = w_ref.shape[1]
    per_row = w_ref.shape[2] // block_size
    if labels:
        section = refs[-4]
        put_shards(me_ref[0], shards, [(*a, r) for a, r in zip(labels, late)], section, sem.at[2])

    half = jnp.asarray(0.5, jnp.bfloat16)

    def copies_out(i):
        return [
            pltpu.make_async_copy(held.at[i], new.at[first + i], sem.at[number, i])
            for number, (held, new) in enumerate(((held_w, new_w_ref), (held_m, new_m_ref)))
        ]

    for i in range(count):
        hid = hid_ref[:, i * block_size : (i + 1) * block_size].T
        for k in range(0, per_row, 2):
            selected = []
            for j in range(2):
                col = cols_ref[k + j, first + i]
                selected.append(section[:, pl.ds(pl.multiple_of(col * block_size, block_size), block_size)])
            gradient = scale * jnp.dot(hid, jnp.concatenate(selected, 1), preferred_element_type=jnp.float32)
            at = (slice(None), slice(k * block_size, (k + 2) * block_size))
            own_w, mate_w = w_ref[i, *at], mate_w_ref[i, *at]
            half_gap = (half * (mate_w - own_w)).astype(jnp.float32)
            mean_w = (half * (own_w + mate_w)).astype(jnp.float32)
            corrected = gradient + LAMBDA_DC * gradient * gradient * half_gap
            moment = (0.5 * MOMENT_DECAY) * (m_ref[i, *at] + mate_m_ref[i, *at]).astype(jnp.float32) + corrected
            held_m[i, *at] = moment.astype(jnp.bfloat16)
            held_w[i, *at] = (mean_w - LEARN_RATE * moment).astype(jnp.bfloat16)
        for copy in copies_out(i):
            copy.start()
    for i in range(count):
        for copy in copies_out(i):
            copy.wait()


def update(me, cols, hidden, weights, momentum, mate_w, mate_m, section, late, scale, shards, first, count, made):
    block_size, width = mate_w.shape[1:]
    mate_first = first if mate_w.shape[0] == weights.shape[0] else 0
    shape = jax.ShapeDtypeStruct(weights.shape, jnp.bfloat16)
    labels, arrays = [a for a, _ in late], [a for _, a in late]
    aliases = {8 + len(arrays) + i: i for i in range(len(made))}
    if late:
        aliases[7] = 2
    held = pltpu.VMEM((count, block_size, width), jnp.bfloat16)
    window = pl.BlockSpec((count, block_size, width), lambda i: (first // count, 0, 0))
    mates = pl.BlockSpec((count, block_size, width), lambda i: (mate_first // count, 0, 0))
    hid = pl.BlockSpec((hidden.shape[0], count * block_size), lambda i: (0, first // count))
    new = pl.pallas_call(
        functools.partial(update_kernel, scale, shards, first, count, labels),
        out_shape=[shape, shape] + [jax.ShapeDtypeStruct(section.shape, section.dtype)] * bool(late),
        grid=(1,),
        in_specs=[IN_SMEM, IN_SMEM, hid, window, window, mates, window, IN_VMEM] + [ANYWHERE] * (len(arrays) + len(made)),
        out_specs=[ANYWHERE, ANYWHERE] + [IN_VMEM] * bool(late),
        scratch_shapes=[held, held, pltpu.SemaphoreType.DMA((3, max(count, len(arrays))))],
        input_output_aliases=aliases,
        compiler_params=pltpu.CompilerParams(vmem_limit_bytes=16 * MIB),
        cost_estimate=LIGHT,
        name="update",
    )(me, cols, hidden, weights, momentum, mate_w, mate_m, section, *arrays, *made)
    return list(new)


def ahead_kernel(scale, first, cols_ref, hid_ref, m_ref, mate_m_ref, section, base_ref, factor_ref):
    count, block_size, width = m_ref.shape
    for i in range(count):
        hid = hid_ref[:, i * block_size : (i + 1) * block_size].T
        for k in range(width // block_size):
            col = cols_ref[k, first + i]
            selected = section[:, pl.ds(pl.multiple_of(col * block_size, block_size), block_size)]
            gradient = scale * jnp.dot(hid, selected, preferred_element_type=jnp.float32)
            at = (i, slice(None), slice(k * block_size, (k + 1) * block_size))
            own_and_mate = (m_ref[at] + mate_m_ref[at]).astype(jnp.float32)
            base_ref[at] = (0.5 * MOMENT_DECAY) * own_and_mate + gradient
            factor_ref[at] = (0.5 * LAMBDA_DC) * gradient * gradient


def update_ahead(cols, hidden, momentum, mate_m, section, scale, first):
    row_blocks, block_size, width = momentum.shape
    count = row_blocks - first
    window = pl.BlockSpec((count, block_size, width), lambda i: (first // count, 0, 0))
    return pl.pallas_call(
        functools.partial(ahead_kernel, scale, first),
        out_shape=[jax.ShapeDtypeStruct((count, block_size, width), jnp.float32)] * 2,
        grid=(1,),
        in_specs=[
            IN_SMEM,
            pl.BlockSpec((hidden.shape[0], count * block_size), lambda i: (0, first // count)),
            window,
            window,
            IN_VMEM,
        ],
        out_specs=[IN_VMEM, IN_VMEM],
        compiler_params=pltpu.CompilerParams(vmem_limit_bytes=8 * MIB),
        cost_estimate=LIGHT,
        name="update_ahead",
    )(cols, hidden, momentum, mate_m, section)


def finish_kernel(first, w_ref, mate_w_ref, base_ref, factor_ref, *refs):
    new_w_ref, new_m_ref, held_w, held_m, sem = refs[-5:]
    count = w_ref.shape[0]
    half = jnp.asarray(0.5, jnp.bfloat16)
    copies = []
    for i in range(count):
        own_w, mate_w = w_ref[i], mate_w_ref[i]
        moment = base_ref[i] + factor_ref[i] * (mate_w - own_w).astype(jnp.float32)
        held_m[i] = moment.astype(jnp.bfloat16)
        mean_w = (half * (own_w + mate_w)).astype(jnp.float32)
        held_w[i] = (mean_w - LEARN_RATE * moment).astype(jnp.bfloat16)
        for number, (held, new) in enumerate(((held_w, new_w_ref), (held_m, new_m_ref))):
            copies.append(pltpu.make_async_copy(held.at[i], new.at[first + i], sem.at[number, i]))
            copies[-1].start()
    for copy in copies:
        copy.wait()


def finish_update(weights, mate_w, base, factor, first, made):
    count, block_size, width = mate_w.shape
    held = pltpu.VMEM(mate_w.shape, jnp.bfloat16)
    shape = jax.ShapeDtypeStruct(weights.shape, jnp.bfloat16)
    return pl.pallas_call(
        functools.partial(finish_kernel, first),
        out_shape=[shape, shape],
        grid=(1,),
        in_specs=[pl.BlockSpec(mate_w.shape, lambda i: (first // count, 0, 0))] + [IN_VMEM] * 3 + [ANYWHERE] * 2,
        out_specs=[ANYWHERE, ANYWHERE],
        scratch_shapes=[held, held, pltpu.SemaphoreType.DMA((2, count))],
        input_output_aliases={4: 0, 5: 1},
        compiler_params=pltpu.CompilerParams(vmem_limit_bytes=8 * MIB),
        cost_estimate=LIGHT,
        name="finish_update",
    )(weights, mate_w, base, factor, *made)


def add_kernel(*refs):
    (*done, own, got_a, got_b, total, held, sem) = refs
    rows = own.shape[0]
    copies = [
        pltpu.make_async_copy(ref, total.at[pl.ds(h * rows, rows)], sem.at[h]) for h, ref in enumerate((*done, held))
    ]
    for copy in copies[:-1]:
        copy.start()
    for r in range(0, rows, 16):
        at = slice(r, r + 16)
        held[at, :] = sum(t[at, :].astype(jnp.float32) for t in (own, got_a, got_b)).astype(jnp.bfloat16)
    copies[-1].start()
    for copy in copies:
        copy.wait()


def add_up(done, terms):
    rows, width = terms[0].shape
    count = len(done) + 1
    return pl.pallas_call(
        add_kernel,
        out_shape=jax.ShapeDtypeStruct((rows * count, width), jnp.bfloat16),
        in_specs=[ANYWHERE] * len(done) + [IN_VMEM] * 3,
        out_specs=pl.BlockSpec(memory_space=pltpu.HBM),
        scratch_shapes=[pltpu.VMEM((rows, width), jnp.bfloat16), pltpu.SemaphoreType.DMA((count,))],
        compiler_params=pltpu.CompilerParams(vmem_limit_bytes=4 * MIB),
        cost_estimate=LIGHT,
        name="add_up",
    )(*done, *terms)


def exchange(value, parity, shards):
    pairs = [(i, i + 1) for i in range(parity, shards - 1, 2)]
    return lax.ppermute(value, "tensor", pairs + [(j, i) for i, j in pairs])


def gather_and_scatter(own, make_parts, after_phase, along, shards, pieces):
    rows = own.shape[0] // pieces
    whole = [exchange(own, side, shards) for side in (0, 1)]
    parts = make_parts()
    whole, parts, along[0] = lax.optimization_barrier((whole, parts, along[0]))
    given = [((0, 0, 0, 1), own)] + [((1, side, 0, 1), whole[side]) for side in (0, 1)]
    got = [[a[h * rows : (h + 1) * rows] for a in whole] for h in range(pieces)]
    for p in range(1, shards):
        for h in range(pieces):
            if p > 1:
                got[h], parts, along[p - 1] = lax.optimization_barrier((got[h], parts, along[p - 1]))
                given += [((p, side, h, pieces), got[h][side]) for side in (0, 1)]
            part = [parts[(2 * p - 1 + side) * pieces + h] for side in (0, 1)]
            got[h] = [exchange(got[h][1 - side] + part[side], side, shards) for side in (0, 1)]
        result = after_phase(p, given, parts)
    totals = []
    for h in range(pieces):
        result, along[shards - 1], got[h] = lax.optimization_barrier((result, along[shards - 1], got[h]))
        if h < pieces - 1:
            totals.append(sum(a.astype(jnp.float32) for a in (parts[h], *got[h])).astype(jnp.bfloat16))
            result, totals = lax.optimization_barrier((result, totals))
    return result, add_up(totals, (parts[pieces - 1], *got[-1]))


def step_for(bit, hidden, out_grad, weights, momentum, block_cols):
    shards = lax.axis_size("tensor")
    replicas = lax.axis_size("replica")
    model_width = out_grad.shape[1]
    scale = (4.0 / (hidden.shape[1] * shards)) ** 0.5
    me = lax.axis_index("tensor").reshape(1).astype(jnp.int32)
    cols = block_cols.T
    row_blocks = weights.shape[0]
    fixed = (me, cols, hidden, weights, momentum)

    def swap(value):
        return lax.ppermute(value, "replica", [(i, i ^ 1 << bit) for i in range(replicas)])

    def forward(pieces):
        return lambda: forward_parts(me, cols, hidden, weights, scale, shards, pieces, model_width)

    along = [[] for _ in range(shards)]
    along[0].append(swap(momentum))
    if bit == 0:
        counted = []

        def beside(p, given, parts):
            if p == 1:
                behind, _ = lax.optimization_barrier((weights, parts[0]))
                along[shards - 2].append(swap(behind))
            if p == shards - 2:
                counted.append(len(given))
                along[p] += start_section(me, shards, given, along[0][0])
            if p == shards - 1:
                (count,), (mate_w, section, mate_m) = counted, along[shards - 2]
                late = given[count:]
                return update(*fixed, mate_w, mate_m, section, late, scale, shards, 0, row_blocks, [])[:2]

        made, outputs = gather_and_scatter(out_grad, forward(2), beside, along, shards, 2)
        return outputs, *made

    cut = row_blocks - rows_per_step(row_blocks)
    head, tail = swap(weights[:cut]), swap(weights[cut:])

    def gathered(p, given, parts):
        return start_section(me, shards, given, along[0][0]) if p == shards - 1 else None

    (section, mate_m), outputs = gather_and_scatter(out_grad, forward(1), gathered, along, shards, 1)
    ahead = update_ahead(cols, hidden, momentum, mate_m, section, scale, cut)
    head, outputs, ahead = lax.optimization_barrier((head, outputs, ahead))
    made = update(*fixed, head, mate_m, section, [], scale, shards, 0, cut, [])
    made = finish_update(weights, tail, *ahead, cut, made)
    return outputs, *made


def body(hidden, out_grad, weights, momentum, block_cols, step_number):
    levels = lax.axis_size("replica").bit_length() - 1
    outputs, new_w, new_m = lax.switch(
        lax.rem(step_number[0], levels),
        [functools.partial(step_for, bit) for bit in range(levels)],
        hidden,
        out_grad,
        weights[0],
        momentum[0],
        block_cols,
    )
    return outputs, new_w[None], new_m[None]


def solution(mesh):
    return jax.shard_map(
        body,
        mesh=mesh,
        in_specs=(
            P("replica", "tensor"),
            P(("replica", "tensor"), None),
            P("replica", "tensor", None, None),
            P("replica", "tensor", None, None),
            P("tensor", None),
            P(),
        ),
        out_specs=(
            P(("replica", "tensor"), None),
            P("replica", "tensor", None, None),
            P("replica", "tensor", None, None),
        ),
        check_vma=False,
    )
```

```python
import functools

import jax
import jax.numpy as jnp
from jax import lax
from jax.experimental import pallas as pl
from jax.experimental.pallas import tpu as pltpu
from jax.sharding import PartitionSpec as P

LAMBDA_DC = 1.0
MOMENT_DECAY = 0.9
LEARN_RATE = 0.2
MIB = 1024 * 1024
LIGHT = pl.CostEstimate(flops=1024, bytes_accessed=1024, transcendentals=0)
ANYWHERE = pl.BlockSpec(memory_space=pl.ANY)
IN_VMEM = pl.BlockSpec(memory_space=pltpu.VMEM)
IN_SMEM = pl.BlockSpec(memory_space=pltpu.SMEM)


def rows_per_step(row_blocks):
    return 2 if row_blocks % 2 == 0 else 1


def forward_kernel(scale, shards, pieces, me_ref, cols_ref, hid_ref, w_ref, *refs):
    parts, total = refs[:-1], refs[-1]
    step = pl.program_id(0)
    rows_step, block_size = w_ref.shape[0], w_ref.shape[1]
    per_row = w_ref.shape[2] // block_size

    @pl.when(step == 0)
    def _():
        total[...] = jnp.zeros_like(total)

    for i in range(rows_step):
        product = jnp.dot(
            hid_ref[:, i * block_size : (i + 1) * block_size],
            w_ref[i],
            preferred_element_type=jnp.float32,
        )
        for k in range(per_row):
            col = cols_ref[k, step * rows_step + i]
            total[col] += product[:, k * block_size : (k + 1) * block_size]

    @pl.when(step == pl.num_programs(0) - 1)
    def _():
        me = me_ref[0]
        even = lax.rem(me, 2) == 0
        below, above = jnp.where(even, me, shards - 1 - me), jnp.where(even, shards - 1 - me, me)
        ahead = jnp.where(even, 1, -1)
        kept = [(me, None)]
        for p in range(1, shards):
            kept += [(me + ahead * (shards - p), below <= p - 1), (me - ahead * (shards - p), above <= p - 1)]
        rows = parts[0].shape[0]
        ends = []
        for number, part in enumerate(parts):
            owner, used = kept[number // pieces]
            factor = scale if used is None else jnp.where(used, scale, 0.0)
            place = jnp.clip(owner, 0, shards - 1) * pieces + number % pieces
            start = pl.multiple_of(place * rows, rows)
            ends.append((part, start, factor))

        def finish(col, _):
            to = pl.ds(pl.multiple_of(col * block_size, block_size), block_size)
            for part, start, factor in ends:
                part[:, to] = (total[col, pl.ds(start, rows), :] * factor).astype(jnp.bfloat16)
            return 0

        lax.fori_loop(0, total.shape[0], finish, 0)


def forward_parts(me, cols, hidden, weights, scale, shards, pieces, model_width):
    tokens = hidden.shape[0]
    row_blocks, block_size, width = weights.shape
    rows_step = rows_per_step(row_blocks)
    rows = tokens // shards // pieces
    count = pieces * (2 * shards - 1)
    return pl.pallas_call(
        functools.partial(forward_kernel, scale, shards, pieces),
        out_shape=[jax.ShapeDtypeStruct((rows, model_width), jnp.bfloat16)] * count,
        grid=(row_blocks // rows_step,),
        in_specs=[
            IN_SMEM,
            IN_SMEM,
            pl.BlockSpec((tokens, rows_step * block_size), lambda r: (0, r)),
            pl.BlockSpec((rows_step, block_size, width), lambda r: (r, 0, 0)),
        ],
        out_specs=[IN_VMEM] * count,
        scratch_shapes=[pltpu.VMEM((model_width // block_size, tokens, block_size), jnp.float32)],
        compiler_params=pltpu.CompilerParams(vmem_limit_bytes=10 * MIB),
        cost_estimate=LIGHT,
        name="forward_parts",
    )(me, cols, hidden, weights)


def put_shards(me, shards, given, section, sem):
    ahead = 1 - 2 * lax.rem(me, 2)
    for act in ("start", "wait"):
        for number, (step, side, piece, pieces, ref) in enumerate(given):
            shard = me + ahead * (step if side == 0 else -step)
            rows = ref.shape[0]

            @pl.when((shard >= 0) & (shard < shards))
            def _(act=act, number=number, piece=piece, pieces=pieces, ref=ref, shard=shard, rows=rows):
                to = section.at[pl.ds(pl.multiple_of((shard * pieces + piece) * rows, rows), rows), :]
                getattr(pltpu.make_async_copy(ref, to, sem.at[number]), act)()


def section_kernel(shards, labels, me_ref, *refs):
    *given, section, sem = refs
    put_shards(me_ref[0], shards, [(*a, r) for a, r in zip(labels, given)], section, sem)


def start_section(me, shards, given):
    labels, arrays = [a for a, _ in given], [a for _, a in given]
    rows, width = arrays[0].shape
    return pl.pallas_call(
        functools.partial(section_kernel, shards, labels),
        out_shape=jax.ShapeDtypeStruct((rows * labels[0][3] * shards, width), jnp.bfloat16),
        in_specs=[IN_SMEM] + [ANYWHERE] * len(arrays),
        out_specs=IN_VMEM,
        scratch_shapes=[pltpu.SemaphoreType.DMA((len(arrays),))],
        compiler_params=pltpu.CompilerParams(vmem_limit_bytes=4 * MIB),
        cost_estimate=LIGHT,
        name="start_section",
    )(me, *arrays)


def stage_kernel(source, staged, sem):
    copy = pltpu.make_async_copy(source, staged, sem)
    copy.start()
    copy.wait()


def stage(array, after):
    array, _ = lax.optimization_barrier((array, after))
    return pl.pallas_call(
        stage_kernel,
        out_shape=jax.ShapeDtypeStruct(array.shape, array.dtype),
        in_specs=[ANYWHERE],
        out_specs=IN_VMEM,
        scratch_shapes=[pltpu.SemaphoreType.DMA],
        compiler_params=pltpu.CompilerParams(vmem_limit_bytes=4 * MIB),
        cost_estimate=LIGHT,
        name="stage",
    )(array)


def update_kernel(scale, shards, first, count, labels, me_ref, cols_ref, hid_ref, w_ref, m_ref, mate_w_ref, mate_m_ref, section, *refs):
    late, (held_w, held_m, sem) = refs[: len(labels)], refs[-3:]
    new_w_ref, new_m_ref = refs[-6:-4] if labels else refs[-5:-3]
    block_size = w_ref.shape[1]
    per_row = w_ref.shape[2] // block_size
    if labels:
        section = refs[-4]
        put_shards(me_ref[0], shards, [(*a, r) for a, r in zip(labels, late)], section, sem.at[2])

    half = jnp.asarray(0.5, jnp.bfloat16)

    def copies_out(i):
        return [
            pltpu.make_async_copy(held.at[i], new.at[first + i], sem.at[number, i])
            for number, (held, new) in enumerate(((held_w, new_w_ref), (held_m, new_m_ref)))
        ]

    for i in range(count):
        hid = hid_ref[:, i * block_size : (i + 1) * block_size].T
        for k in range(0, per_row, 2):
            selected = []
            for j in range(2):
                col = cols_ref[k + j, first + i]
                selected.append(section[:, pl.ds(pl.multiple_of(col * block_size, block_size), block_size)])
            gradient = scale * jnp.dot(hid, jnp.concatenate(selected, 1), preferred_element_type=jnp.float32)
            at = (slice(None), slice(k * block_size, (k + 2) * block_size))
            own_w, mate_w = w_ref[i, *at], mate_w_ref[i, *at]
            half_gap = (half * (mate_w - own_w)).astype(jnp.float32)
            mean_w = (half * (own_w + mate_w)).astype(jnp.float32)
            corrected = gradient + LAMBDA_DC * gradient * gradient * half_gap
            moment = (0.5 * MOMENT_DECAY) * (m_ref[i, *at] + mate_m_ref[i, *at]).astype(jnp.float32) + corrected
            held_m[i, *at] = moment.astype(jnp.bfloat16)
            held_w[i, *at] = (mean_w - LEARN_RATE * moment).astype(jnp.bfloat16)
        for copy in copies_out(i):
            copy.start()
    for i in range(count):
        for copy in copies_out(i):
            copy.wait()


def update(me, cols, hidden, weights, momentum, mate_w, mate_m, section, late, scale, shards, first, count, made):
    block_size, width = mate_w.shape[1:]
    mate_first = first if mate_w.shape[0] == weights.shape[0] else 0
    shape = jax.ShapeDtypeStruct(weights.shape, jnp.bfloat16)
    labels, arrays = [a for a, _ in late], [a for _, a in late]
    aliases = {8 + len(arrays) + i: i for i in range(len(made))}
    if late:
        aliases[7] = 2
    held = pltpu.VMEM((count, block_size, width), jnp.bfloat16)
    window = pl.BlockSpec((count, block_size, width), lambda i: (first // count, 0, 0))
    mates = pl.BlockSpec((count, block_size, width), lambda i: (mate_first // count, 0, 0))
    hid = pl.BlockSpec((hidden.shape[0], count * block_size), lambda i: (0, first // count))
    new = pl.pallas_call(
        functools.partial(update_kernel, scale, shards, first, count, labels),
        out_shape=[shape, shape] + [jax.ShapeDtypeStruct(section.shape, section.dtype)] * bool(late),
        grid=(1,),
        in_specs=[IN_SMEM, IN_SMEM, hid, window, window, mates, window, IN_VMEM] + [ANYWHERE] * (len(arrays) + len(made)),
        out_specs=[ANYWHERE, ANYWHERE] + [IN_VMEM] * bool(late),
        scratch_shapes=[held, held, pltpu.SemaphoreType.DMA((3, max(count, len(arrays))))],
        input_output_aliases=aliases,
        compiler_params=pltpu.CompilerParams(vmem_limit_bytes=16 * MIB),
        cost_estimate=LIGHT,
        name="update",
    )(me, cols, hidden, weights, momentum, mate_w, mate_m, section, *arrays, *made)
    return list(new)


def ahead_kernel(scale, first, cols_ref, hid_ref, m_ref, mate_m_ref, section, base_ref, factor_ref):
    count, block_size, width = m_ref.shape
    for i in range(count):
        hid = hid_ref[:, i * block_size : (i + 1) * block_size].T
        for k in range(width // block_size):
            col = cols_ref[k, first + i]
            selected = section[:, pl.ds(pl.multiple_of(col * block_size, block_size), block_size)]
            gradient = scale * jnp.dot(hid, selected, preferred_element_type=jnp.float32)
            at = (i, slice(None), slice(k * block_size, (k + 1) * block_size))
            own_and_mate = (m_ref[at] + mate_m_ref[at]).astype(jnp.float32)
            base_ref[at] = (0.5 * MOMENT_DECAY) * own_and_mate + gradient
            factor_ref[at] = (0.5 * LAMBDA_DC) * gradient * gradient


def update_ahead(cols, hidden, momentum, mate_m, section, scale, first):
    row_blocks, block_size, width = momentum.shape
    count = row_blocks - first
    window = pl.BlockSpec((count, block_size, width), lambda i: (first // count, 0, 0))
    return pl.pallas_call(
        functools.partial(ahead_kernel, scale, first),
        out_shape=[jax.ShapeDtypeStruct((count, block_size, width), jnp.float32)] * 2,
        grid=(1,),
        in_specs=[
            IN_SMEM,
            pl.BlockSpec((hidden.shape[0], count * block_size), lambda i: (0, first // count)),
            window,
            window,
            IN_VMEM,
        ],
        out_specs=[IN_VMEM, IN_VMEM],
        compiler_params=pltpu.CompilerParams(vmem_limit_bytes=8 * MIB),
        cost_estimate=LIGHT,
        name="update_ahead",
    )(cols, hidden, momentum, mate_m, section)


def finish_kernel(first, w_ref, mate_w_ref, base_ref, factor_ref, *refs):
    new_w_ref, new_m_ref, held_w, held_m, sem = refs[-5:]
    count = w_ref.shape[0]
    half = jnp.asarray(0.5, jnp.bfloat16)
    copies = []
    for i in range(count):
        own_w, mate_w = w_ref[i], mate_w_ref[i]
        moment = base_ref[i] + factor_ref[i] * (mate_w - own_w).astype(jnp.float32)
        held_m[i] = moment.astype(jnp.bfloat16)
        mean_w = (half * (own_w + mate_w)).astype(jnp.float32)
        held_w[i] = (mean_w - LEARN_RATE * moment).astype(jnp.bfloat16)
        for number, (held, new) in enumerate(((held_w, new_w_ref), (held_m, new_m_ref))):
            copies.append(pltpu.make_async_copy(held.at[i], new.at[first + i], sem.at[number, i]))
            copies[-1].start()
    for copy in copies:
        copy.wait()


def finish_update(weights, mate_w, base, factor, first, made):
    count, block_size, width = mate_w.shape
    held = pltpu.VMEM(mate_w.shape, jnp.bfloat16)
    shape = jax.ShapeDtypeStruct(weights.shape, jnp.bfloat16)
    return pl.pallas_call(
        functools.partial(finish_kernel, first),
        out_shape=[shape, shape],
        grid=(1,),
        in_specs=[pl.BlockSpec(mate_w.shape, lambda i: (first // count, 0, 0))] + [IN_VMEM] * 3 + [ANYWHERE] * 2,
        out_specs=[ANYWHERE, ANYWHERE],
        scratch_shapes=[held, held, pltpu.SemaphoreType.DMA((2, count))],
        input_output_aliases={4: 0, 5: 1},
        compiler_params=pltpu.CompilerParams(vmem_limit_bytes=8 * MIB),
        cost_estimate=LIGHT,
        name="finish_update",
    )(weights, mate_w, base, factor, *made)


def add_kernel(*refs):
    (*done, own, got_a, got_b, total, held, sem) = refs
    rows = own.shape[0]
    copies = [
        pltpu.make_async_copy(ref, total.at[pl.ds(h * rows, rows)], sem.at[h]) for h, ref in enumerate((*done, held))
    ]
    for copy in copies[:-1]:
        copy.start()
    for r in range(0, rows, 16):
        at = slice(r, r + 16)
        held[at, :] = sum(t[at, :].astype(jnp.float32) for t in (own, got_a, got_b)).astype(jnp.bfloat16)
    copies[-1].start()
    for copy in copies:
        copy.wait()


def add_up(done, terms):
    rows, width = terms[0].shape
    count = len(done) + 1
    return pl.pallas_call(
        add_kernel,
        out_shape=jax.ShapeDtypeStruct((rows * count, width), jnp.bfloat16),
        in_specs=[ANYWHERE] * len(done) + [IN_VMEM] * 3,
        out_specs=pl.BlockSpec(memory_space=pltpu.HBM),
        scratch_shapes=[pltpu.VMEM((rows, width), jnp.bfloat16), pltpu.SemaphoreType.DMA((count,))],
        compiler_params=pltpu.CompilerParams(vmem_limit_bytes=4 * MIB),
        cost_estimate=LIGHT,
        name="add_up",
    )(*done, *terms)


def exchange(value, parity, shards):
    pairs = [(i, i + 1) for i in range(parity, shards - 1, 2)]
    return lax.ppermute(value, "tensor", pairs + [(j, i) for i, j in pairs])


def gather_and_scatter(own, make_parts, after_phase, along, shards, pieces):
    rows = own.shape[0] // pieces
    whole = [exchange(own, side, shards) for side in (0, 1)]
    parts = make_parts()
    whole, parts, along[0] = lax.optimization_barrier((whole, parts, along[0]))
    given = [((0, 0, 0, 1), own)] + [((1, side, 0, 1), whole[side]) for side in (0, 1)]
    got = [[a[h * rows : (h + 1) * rows] for a in whole] for h in range(pieces)]
    for p in range(1, shards):
        for h in range(pieces):
            if p > 1:
                got[h], parts, along[p - 1] = lax.optimization_barrier((got[h], parts, along[p - 1]))
                given += [((p, side, h, pieces), got[h][side]) for side in (1, 0)]
            part = [parts[(2 * p - 1 + side) * pieces + h] for side in (0, 1)]
            got[h] = [exchange(got[h][1 - side] + part[side], side, shards) for side in (0, 1)]
        result = after_phase(p, given, parts)
    totals = []
    for h in range(pieces):
        result, along[shards - 1], got[h] = lax.optimization_barrier((result, along[shards - 1], got[h]))
        if h < pieces - 1:
            totals.append(sum(a.astype(jnp.float32) for a in (parts[h], *got[h])).astype(jnp.bfloat16))
            result, totals = lax.optimization_barrier((result, totals))
    return result, add_up(totals, (parts[pieces - 1], *got[-1]))


def step_for(bit, hidden, out_grad, weights, momentum, block_cols):
    shards = lax.axis_size("tensor")
    replicas = lax.axis_size("replica")
    model_width = out_grad.shape[1]
    scale = (4.0 / (hidden.shape[1] * shards)) ** 0.5
    me = lax.axis_index("tensor").reshape(1).astype(jnp.int32)
    cols = block_cols.T
    row_blocks = weights.shape[0]
    fixed = (me, cols, hidden, weights, momentum)

    def swap(value):
        return lax.ppermute(value, "replica", [(i, i ^ 1 << bit) for i in range(replicas)])

    def forward(pieces):
        return lambda: forward_parts(me, cols, hidden, weights, scale, shards, pieces, model_width)

    along = [[] for _ in range(shards)]
    along[0].append(swap(momentum))
    if bit == 0:
        counted = []

        def parts_then_stage():
            parts = forward(2)()
            along[0][0] = stage(along[0][0], parts[0])
            return parts

        def beside(p, given, parts):
            if p == 1:
                behind, _ = lax.optimization_barrier((weights, parts[0]))
                along[shards - 2].append(swap(behind))
            if p == shards - 2:
                counted.append(len(given))
                along[p].append(start_section(me, shards, given))
            if p == shards - 1:
                (count,), (mate_m,), (mate_w, section) = counted, along[0], along[shards - 2]
                late = given[count:]
                return update(*fixed, mate_w, mate_m, section, late, scale, shards, 0, row_blocks, [])[:2]

        made, outputs = gather_and_scatter(out_grad, parts_then_stage, beside, along, shards, 2)
        return outputs, *made

    cut = row_blocks - rows_per_step(row_blocks)
    head, tail = swap(weights[:cut]), swap(weights[cut:])

    def gathered(p, given, parts):
        return start_section(me, shards, given) if p == shards - 1 else None

    section, outputs = gather_and_scatter(out_grad, forward(1), gathered, along, shards, 1)
    mate_m = stage(along[0][0], section)
    ahead = update_ahead(cols, hidden, momentum, mate_m, section, scale, cut)
    head, outputs, ahead = lax.optimization_barrier((head, outputs, ahead))
    made = update(*fixed, head, mate_m, section, [], scale, shards, 0, cut, [])
    made = finish_update(weights, tail, *ahead, cut, made)
    return outputs, *made


def body(hidden, out_grad, weights, momentum, block_cols, step_number):
    levels = lax.axis_size("replica").bit_length() - 1
    outputs, new_w, new_m = lax.switch(
        lax.rem(step_number[0], levels),
        [functools.partial(step_for, bit) for bit in range(levels)],
        hidden,
        out_grad,
        weights[0],
        momentum[0],
        block_cols,
    )
    return outputs, new_w[None], new_m[None]


def solution(mesh):
    return jax.shard_map(
        body,
        mesh=mesh,
        in_specs=(
            P("replica", "tensor"),
            P(("replica", "tensor"), None),
            P("replica", "tensor", None, None),
            P("replica", "tensor", None, None),
            P("tensor", None),
            P(),
        ),
        out_specs=(
            P(("replica", "tensor"), None),
            P("replica", "tensor", None, None),
            P("replica", "tensor", None, None),
        ),
        check_vma=False,
    )
```

```python
import functools

import jax
import jax.numpy as jnp
from jax import lax
from jax.experimental import pallas as pl
from jax.experimental.pallas import tpu as pltpu
from jax.sharding import PartitionSpec as P

LAMBDA_DC = 1.0
MOMENT_DECAY = 0.9
LEARN_RATE = 0.2
MIB = 1024 * 1024
LIGHT = pl.CostEstimate(flops=1024, bytes_accessed=1024, transcendentals=0)
ANYWHERE = pl.BlockSpec(memory_space=pl.ANY)
IN_VMEM = pl.BlockSpec(memory_space=pltpu.VMEM)
IN_SMEM = pl.BlockSpec(memory_space=pltpu.SMEM)


def rows_per_step(row_blocks):
    return 2 if row_blocks % 2 == 0 else 1


def forward_kernel(scale, shards, pieces, me_ref, cols_ref, hid_ref, w_ref, *refs):
    parts, total = refs[:-1], refs[-1]
    step = pl.program_id(0)
    rows_step, block_size = w_ref.shape[0], w_ref.shape[1]
    per_row = w_ref.shape[2] // block_size

    @pl.when(step == 0)
    def _():
        total[...] = jnp.zeros_like(total)

    for i in range(rows_step):
        product = jnp.dot(
            hid_ref[:, i * block_size : (i + 1) * block_size],
            w_ref[i],
            preferred_element_type=jnp.float32,
        )
        for k in range(per_row):
            col = cols_ref[k, step * rows_step + i]
            total[col] += product[:, k * block_size : (k + 1) * block_size]

    @pl.when(step == pl.num_programs(0) - 1)
    def _():
        me = me_ref[0]
        even = lax.rem(me, 2) == 0
        below, above = jnp.where(even, me, shards - 1 - me), jnp.where(even, shards - 1 - me, me)
        ahead = jnp.where(even, 1, -1)
        kept = [(me, None)]
        for p in range(1, shards):
            kept += [(me + ahead * (shards - p), below <= p - 1), (me - ahead * (shards - p), above <= p - 1)]
        rows = parts[0].shape[0]
        ends = []
        for number, part in enumerate(parts):
            owner, used = kept[number // pieces]
            factor = scale if used is None else jnp.where(used, scale, 0.0)
            place = jnp.clip(owner, 0, shards - 1) * pieces + number % pieces
            start = pl.multiple_of(place * rows, rows)
            ends.append((part, start, factor))

        def finish(col, _):
            to = pl.ds(pl.multiple_of(col * block_size, block_size), block_size)
            for part, start, factor in ends:
                part[:, to] = (total[col, pl.ds(start, rows), :] * factor).astype(jnp.bfloat16)
            return 0

        lax.fori_loop(0, total.shape[0], finish, 0)


def forward_parts(me, cols, hidden, weights, scale, shards, pieces, model_width):
    tokens = hidden.shape[0]
    row_blocks, block_size, width = weights.shape
    rows_step = row_blocks // 2 if row_blocks % 2 == 0 else 1
    rows = tokens // shards // pieces
    count = pieces * (2 * shards - 1)
    return pl.pallas_call(
        functools.partial(forward_kernel, scale, shards, pieces),
        out_shape=[jax.ShapeDtypeStruct((rows, model_width), jnp.bfloat16)] * count,
        grid=(row_blocks // rows_step,),
        in_specs=[
            IN_SMEM,
            IN_SMEM,
            pl.BlockSpec((tokens, rows_step * block_size), lambda r: (0, r)),
            pl.BlockSpec((rows_step, block_size, width), lambda r: (r, 0, 0)),
        ],
        out_specs=[IN_VMEM] * count,
        scratch_shapes=[pltpu.VMEM((model_width // block_size, tokens, block_size), jnp.float32)],
        compiler_params=pltpu.CompilerParams(vmem_limit_bytes=10 * MIB),
        cost_estimate=LIGHT,
        name="forward_parts",
    )(me, cols, hidden, weights)


def put_shards(me, shards, given, section, sem):
    ahead = 1 - 2 * lax.rem(me, 2)
    for act in ("start", "wait"):
        for number, (step, side, piece, pieces, ref) in enumerate(given):
            shard = me + ahead * (step if side == 0 else -step)
            rows = ref.shape[0]

            @pl.when((shard >= 0) & (shard < shards))
            def _(act=act, number=number, piece=piece, pieces=pieces, ref=ref, shard=shard, rows=rows):
                to = section.at[pl.ds(pl.multiple_of((shard * pieces + piece) * rows, rows), rows), :]
                getattr(pltpu.make_async_copy(ref, to, sem.at[number]), act)()


def section_kernel(shards, labels, me_ref, *refs):
    *given, section, sem = refs
    put_shards(me_ref[0], shards, [(*a, r) for a, r in zip(labels, given)], section, sem)


def start_section(me, shards, given):
    labels, arrays = [a for a, _ in given], [a for _, a in given]
    rows, width = arrays[0].shape
    return pl.pallas_call(
        functools.partial(section_kernel, shards, labels),
        out_shape=jax.ShapeDtypeStruct((rows * labels[0][3] * shards, width), jnp.bfloat16),
        in_specs=[IN_SMEM] + [ANYWHERE] * len(arrays),
        out_specs=IN_VMEM,
        scratch_shapes=[pltpu.SemaphoreType.DMA((len(arrays),))],
        compiler_params=pltpu.CompilerParams(vmem_limit_bytes=4 * MIB),
        cost_estimate=LIGHT,
        name="start_section",
    )(me, *arrays)


def mix_kernel(own_ref, mate_ref, mixed_ref):
    count = own_ref.shape[0]
    for i in range(count):
        both = own_ref[i].astype(jnp.float32) + mate_ref[i].astype(jnp.float32)
        mixed_ref[pl.program_id(0) * count + i] = ((0.5 * MOMENT_DECAY) * both).astype(jnp.bfloat16)


def mix_momentum(momentum, mate_m, after):
    mate_m, _ = lax.optimization_barrier((mate_m, after))
    row_blocks, block_size, width = momentum.shape
    count = row_blocks // 2 if row_blocks % 2 == 0 else 1
    window = pl.BlockSpec((count, block_size, width), lambda i: (i, 0, 0))
    return pl.pallas_call(
        mix_kernel,
        out_shape=jax.ShapeDtypeStruct(momentum.shape, jnp.bfloat16),
        grid=(row_blocks // count,),
        in_specs=[window, window],
        out_specs=IN_VMEM,
        compiler_params=pltpu.CompilerParams(vmem_limit_bytes=10 * MIB),
        cost_estimate=LIGHT,
        name="mix_momentum",
    )(momentum, mate_m)


def update_kernel(scale, shards, first, count, labels, me_ref, cols_ref, hid_ref, w_ref, mate_w_ref, mixed_ref, section, *refs):
    late, (held_w, held_m, sem) = refs[: len(labels)], refs[-3:]
    new_w_ref, new_m_ref = refs[-6:-4] if labels else refs[-5:-3]
    block_size = w_ref.shape[1]
    per_row = w_ref.shape[2] // block_size
    if labels:
        section = refs[-4]
        put_shards(me_ref[0], shards, [(*a, r) for a, r in zip(labels, late)], section, sem.at[2])

    half = jnp.asarray(0.5, jnp.bfloat16)

    def copies_out(i):
        return [
            pltpu.make_async_copy(held.at[i], new.at[first + i], sem.at[number, i])
            for number, (held, new) in enumerate(((held_w, new_w_ref), (held_m, new_m_ref)))
        ]

    for i in range(count):
        hid = hid_ref[:, i * block_size : (i + 1) * block_size].T
        for k in range(0, per_row, 2):
            selected = []
            for j in range(2):
                col = cols_ref[k + j, first + i]
                selected.append(section[:, pl.ds(pl.multiple_of(col * block_size, block_size), block_size)])
            gradient = scale * jnp.dot(hid, jnp.concatenate(selected, 1), preferred_element_type=jnp.float32)
            at = (slice(None), slice(k * block_size, (k + 2) * block_size))
            own_w, mate_w = w_ref[i, *at], mate_w_ref[i, *at]
            half_gap = (half * (mate_w - own_w)).astype(jnp.float32)
            mean_w = (half * (own_w + mate_w)).astype(jnp.float32)
            corrected = gradient + LAMBDA_DC * gradient * gradient * half_gap
            moment = mixed_ref[i, *at].astype(jnp.float32) + corrected
            held_m[i, *at] = moment.astype(jnp.bfloat16)
            held_w[i, *at] = (mean_w - LEARN_RATE * moment).astype(jnp.bfloat16)
        for copy in copies_out(i):
            copy.start()
    for i in range(count):
        for copy in copies_out(i):
            copy.wait()


def update(me, cols, hidden, weights, mate_w, mixed, section, late, scale, shards, first, count, made):
    block_size, width = mate_w.shape[1:]
    mate_first = first if mate_w.shape[0] == weights.shape[0] else 0
    shape = jax.ShapeDtypeStruct(weights.shape, jnp.bfloat16)
    labels, arrays = [a for a, _ in late], [a for _, a in late]
    aliases = {7 + len(arrays) + i: i for i in range(len(made))}
    if late:
        aliases[6] = 2
    held = pltpu.VMEM((count, block_size, width), jnp.bfloat16)
    window = pl.BlockSpec((count, block_size, width), lambda i: (first // count, 0, 0))
    mates = pl.BlockSpec((count, block_size, width), lambda i: (mate_first // count, 0, 0))
    hid = pl.BlockSpec((hidden.shape[0], count * block_size), lambda i: (0, first // count))
    new = pl.pallas_call(
        functools.partial(update_kernel, scale, shards, first, count, labels),
        out_shape=[shape, shape] + [jax.ShapeDtypeStruct(section.shape, section.dtype)] * bool(late),
        grid=(1,),
        in_specs=[IN_SMEM, IN_SMEM, hid, window, mates, window, IN_VMEM] + [ANYWHERE] * (len(arrays) + len(made)),
        out_specs=[ANYWHERE, ANYWHERE] + [IN_VMEM] * bool(late),
        scratch_shapes=[held, held, pltpu.SemaphoreType.DMA((3, max(count, len(arrays))))],
        input_output_aliases=aliases,
        compiler_params=pltpu.CompilerParams(vmem_limit_bytes=16 * MIB),
        cost_estimate=LIGHT,
        name="update",
    )(me, cols, hidden, weights, mate_w, mixed, section, *arrays, *made)
    return list(new)


def ahead_kernel(scale, first, cols_ref, hid_ref, mixed_ref, section, base_ref, factor_ref):
    count, block_size, width = mixed_ref.shape
    for i in range(count):
        hid = hid_ref[:, i * block_size : (i + 1) * block_size].T
        for k in range(width // block_size):
            col = cols_ref[k, first + i]
            selected = section[:, pl.ds(pl.multiple_of(col * block_size, block_size), block_size)]
            gradient = scale * jnp.dot(hid, selected, preferred_element_type=jnp.float32)
            at = (i, slice(None), slice(k * block_size, (k + 1) * block_size))
            base_ref[at] = mixed_ref[at].astype(jnp.float32) + gradient
            factor_ref[at] = (0.5 * LAMBDA_DC) * gradient * gradient


def update_ahead(cols, hidden, mixed, section, scale, first):
    row_blocks, block_size, width = mixed.shape
    count = row_blocks - first
    window = pl.BlockSpec((count, block_size, width), lambda i: (first // count, 0, 0))
    return pl.pallas_call(
        functools.partial(ahead_kernel, scale, first),
        out_shape=[jax.ShapeDtypeStruct((count, block_size, width), jnp.float32)] * 2,
        grid=(1,),
        in_specs=[
            IN_SMEM,
            pl.BlockSpec((hidden.shape[0], count * block_size), lambda i: (0, first // count)),
            window,
            IN_VMEM,
        ],
        out_specs=[IN_VMEM, IN_VMEM],
        compiler_params=pltpu.CompilerParams(vmem_limit_bytes=8 * MIB),
        cost_estimate=LIGHT,
        name="update_ahead",
    )(cols, hidden, mixed, section)


def finish_kernel(first, w_ref, mate_w_ref, base_ref, factor_ref, *refs):
    new_w_ref, new_m_ref, held_w, held_m, sem = refs[-5:]
    count = w_ref.shape[0]
    half = jnp.asarray(0.5, jnp.bfloat16)
    copies = []
    for i in range(count):
        own_w, mate_w = w_ref[i], mate_w_ref[i]
        moment = base_ref[i] + factor_ref[i] * (mate_w - own_w).astype(jnp.float32)
        held_m[i] = moment.astype(jnp.bfloat16)
        mean_w = (half * (own_w + mate_w)).astype(jnp.float32)
        held_w[i] = (mean_w - LEARN_RATE * moment).astype(jnp.bfloat16)
        for number, (held, new) in enumerate(((held_w, new_w_ref), (held_m, new_m_ref))):
            copies.append(pltpu.make_async_copy(held.at[i], new.at[first + i], sem.at[number, i]))
            copies[-1].start()
    for copy in copies:
        copy.wait()


def finish_update(weights, mate_w, base, factor, first, made):
    count, block_size, width = mate_w.shape
    held = pltpu.VMEM(mate_w.shape, jnp.bfloat16)
    shape = jax.ShapeDtypeStruct(weights.shape, jnp.bfloat16)
    return pl.pallas_call(
        functools.partial(finish_kernel, first),
        out_shape=[shape, shape],
        grid=(1,),
        in_specs=[pl.BlockSpec(mate_w.shape, lambda i: (first // count, 0, 0))] + [IN_VMEM] * 3 + [ANYWHERE] * 2,
        out_specs=[ANYWHERE, ANYWHERE],
        scratch_shapes=[held, held, pltpu.SemaphoreType.DMA((2, count))],
        input_output_aliases={4: 0, 5: 1},
        compiler_params=pltpu.CompilerParams(vmem_limit_bytes=8 * MIB),
        cost_estimate=LIGHT,
        name="finish_update",
    )(weights, mate_w, base, factor, *made)


def add_kernel(*refs):
    (*done, own, got_a, got_b, total, held, sem) = refs
    rows = own.shape[0]
    copies = [
        pltpu.make_async_copy(ref, total.at[pl.ds(h * rows, rows)], sem.at[h]) for h, ref in enumerate((*done, held))
    ]
    for copy in copies[:-1]:
        copy.start()
    for r in range(0, rows, 16):
        at = slice(r, r + 16)
        held[at, :] = sum(t[at, :].astype(jnp.float32) for t in (own, got_a, got_b)).astype(jnp.bfloat16)
    copies[-1].start()
    for copy in copies:
        copy.wait()


def add_up(done, terms):
    rows, width = terms[0].shape
    count = len(done) + 1
    return pl.pallas_call(
        add_kernel,
        out_shape=jax.ShapeDtypeStruct((rows * count, width), jnp.bfloat16),
        in_specs=[ANYWHERE] * len(done) + [IN_VMEM] * 3,
        out_specs=pl.BlockSpec(memory_space=pltpu.HBM),
        scratch_shapes=[pltpu.VMEM((rows, width), jnp.bfloat16), pltpu.SemaphoreType.DMA((count,))],
        compiler_params=pltpu.CompilerParams(vmem_limit_bytes=4 * MIB),
        cost_estimate=LIGHT,
        name="add_up",
    )(*done, *terms)


def exchange(value, parity, shards):
    pairs = [(i, i + 1) for i in range(parity, shards - 1, 2)]
    return lax.ppermute(value, "tensor", pairs + [(j, i) for i, j in pairs])


def gather_and_scatter(own, make_parts, after_phase, along, shards, pieces):
    rows = own.shape[0] // pieces
    whole = [exchange(own, side, shards) for side in (0, 1)]
    parts = make_parts()
    whole, parts, along[0] = lax.optimization_barrier((whole, parts, along[0]))
    given = [((0, 0, 0, 1), own)] + [((1, side, 0, 1), whole[side]) for side in (0, 1)]
    got = [[a[h * rows : (h + 1) * rows] for a in whole] for h in range(pieces)]
    for p in range(1, shards):
        for h in range(pieces):
            if p > 1:
                got[h], parts, along[p - 1] = lax.optimization_barrier((got[h], parts, along[p - 1]))
                given += [((p, side, h, pieces), got[h][side]) for side in (1, 0)]
            part = [parts[(2 * p - 1 + side) * pieces + h] for side in (0, 1)]
            got[h] = [exchange(got[h][1 - side] + part[side], side, shards) for side in (0, 1)]
        result = after_phase(p, given, parts)
    totals = []
    for h in range(pieces):
        result, along[shards - 1], got[h] = lax.optimization_barrier((result, along[shards - 1], got[h]))
        if h < pieces - 1:
            totals.append(sum(a.astype(jnp.float32) for a in (parts[h], *got[h])).astype(jnp.bfloat16))
            result, totals = lax.optimization_barrier((result, totals))
    return result, add_up(totals, (parts[pieces - 1], *got[-1]))


def step_for(bit, hidden, out_grad, weights, momentum, block_cols):
    shards = lax.axis_size("tensor")
    replicas = lax.axis_size("replica")
    model_width = out_grad.shape[1]
    scale = (4.0 / (hidden.shape[1] * shards)) ** 0.5
    me = lax.axis_index("tensor").reshape(1).astype(jnp.int32)
    cols = block_cols.T
    row_blocks = weights.shape[0]
    fixed = (me, cols, hidden, weights)

    def swap(value):
        return lax.ppermute(value, "replica", [(i, i ^ 1 << bit) for i in range(replicas)])

    def forward(pieces):
        return lambda: forward_parts(me, cols, hidden, weights, scale, shards, pieces, model_width)

    along = [[] for _ in range(shards)]
    along[0].append(swap(momentum))
    if bit == 0:
        counted = []

        def parts_then_mix():
            parts = forward(2)()
            along[0][0] = mix_momentum(momentum, along[0][0], parts[0])
            return parts

        def beside(p, given, parts):
            if p == 1:
                behind, _ = lax.optimization_barrier((weights, parts[0]))
                along[shards - 2].append(swap(behind))
            if p == shards - 2:
                counted.append(len(given))
                along[p].append(start_section(me, shards, given))
            if p == shards - 1:
                (count,), (mixed,), (mate_w, section) = counted, along[0], along[shards - 2]
                late = given[count:]
                return update(*fixed, mate_w, mixed, section, late, scale, shards, 0, row_blocks, [])[:2]

        made, outputs = gather_and_scatter(out_grad, parts_then_mix, beside, along, shards, 2)
        return outputs, *made

    cut = row_blocks - rows_per_step(row_blocks)
    head, tail = swap(weights[:cut]), swap(weights[cut:])

    def gathered(p, given, parts):
        return start_section(me, shards, given) if p == shards - 1 else None

    section, outputs = gather_and_scatter(out_grad, forward(1), gathered, along, shards, 1)
    mixed = mix_momentum(momentum, along[0][0], section)
    ahead = update_ahead(cols, hidden, mixed, section, scale, cut)
    head, outputs, ahead = lax.optimization_barrier((head, outputs, ahead))
    made = update(*fixed, head, mixed, section, [], scale, shards, 0, cut, [])
    made = finish_update(weights, tail, *ahead, cut, made)
    return outputs, *made


def body(hidden, out_grad, weights, momentum, block_cols, step_number):
    levels = lax.axis_size("replica").bit_length() - 1
    outputs, new_w, new_m = lax.switch(
        lax.rem(step_number[0], levels),
        [functools.partial(step_for, bit) for bit in range(levels)],
        hidden,
        out_grad,
        weights[0],
        momentum[0],
        block_cols,
    )
    return outputs, new_w[None], new_m[None]


def solution(mesh):
    return jax.shard_map(
        body,
        mesh=mesh,
        in_specs=(
            P("replica", "tensor"),
            P(("replica", "tensor"), None),
            P("replica", "tensor", None, None),
            P("replica", "tensor", None, None),
            P("tensor", None),
            P(),
        ),
        out_specs=(
            P(("replica", "tensor"), None),
            P("replica", "tensor", None, None),
            P("replica", "tensor", None, None),
        ),
        check_vma=False,
    )
```

```python
import functools

import jax
import jax.numpy as jnp
from jax import lax
from jax.experimental import pallas as pl
from jax.experimental.pallas import tpu as pltpu
from jax.sharding import PartitionSpec as P

LAMBDA_DC = 1.0
MOMENT_DECAY = 0.9
LEARN_RATE = 0.2
MIB = 1024 * 1024
LIGHT = pl.CostEstimate(flops=1024, bytes_accessed=1024, transcendentals=0)
ANYWHERE = pl.BlockSpec(memory_space=pl.ANY)
IN_VMEM = pl.BlockSpec(memory_space=pltpu.VMEM)
IN_SMEM = pl.BlockSpec(memory_space=pltpu.SMEM)


def rows_per_step(row_blocks):
    return 2 if row_blocks % 2 == 0 else 1


def forward_kernel(scale, shards, pieces, me_ref, cols_ref, hid_ref, w_ref, *refs):
    parts, total = refs[:-1], refs[-1]
    step = pl.program_id(0)
    rows_step, block_size = w_ref.shape[0], w_ref.shape[1]
    per_row = w_ref.shape[2] // block_size

    @pl.when(step == 0)
    def _():
        total[...] = jnp.zeros_like(total)

    for i in range(rows_step):
        product = jnp.dot(
            hid_ref[:, i * block_size : (i + 1) * block_size],
            w_ref[i],
            preferred_element_type=jnp.float32,
        )
        for k in range(per_row):
            col = cols_ref[k, step * rows_step + i]
            total[col] += product[:, k * block_size : (k + 1) * block_size]

    @pl.when(step == pl.num_programs(0) - 1)
    def _():
        me = me_ref[0]
        even = lax.rem(me, 2) == 0
        below, above = jnp.where(even, me, shards - 1 - me), jnp.where(even, shards - 1 - me, me)
        ahead = jnp.where(even, 1, -1)
        kept = [(me, None)]
        for p in range(1, shards):
            kept += [(me + ahead * (shards - p), below <= p - 1), (me - ahead * (shards - p), above <= p - 1)]
        rows = parts[0].shape[0]
        ends = []
        for number, part in enumerate(parts):
            owner, used = kept[number // pieces]
            factor = scale if used is None else jnp.where(used, scale, 0.0)
            place = jnp.clip(owner, 0, shards - 1) * pieces + number % pieces
            start = pl.multiple_of(place * rows, rows)
            ends.append((part, start, factor))

        def finish(col, _):
            to = pl.ds(pl.multiple_of(col * block_size, block_size), block_size)
            for part, start, factor in ends:
                part[:, to] = (total[col, pl.ds(start, rows), :] * factor).astype(jnp.bfloat16)
            return 0

        lax.fori_loop(0, total.shape[0], finish, 0)


def forward_parts(me, cols, hidden, weights, scale, shards, pieces, model_width):
    tokens = hidden.shape[0]
    row_blocks, block_size, width = weights.shape
    rows_step = row_blocks // 2 if row_blocks % 2 == 0 else 1
    rows = tokens // shards // pieces
    count = pieces * (2 * shards - 1)
    return pl.pallas_call(
        functools.partial(forward_kernel, scale, shards, pieces),
        out_shape=[jax.ShapeDtypeStruct((rows, model_width), jnp.bfloat16)] * count,
        grid=(row_blocks // rows_step,),
        in_specs=[
            IN_SMEM,
            IN_SMEM,
            pl.BlockSpec((tokens, rows_step * block_size), lambda r: (0, r)),
            pl.BlockSpec((rows_step, block_size, width), lambda r: (r, 0, 0)),
        ],
        out_specs=[IN_VMEM] * count,
        scratch_shapes=[pltpu.VMEM((model_width // block_size, tokens, block_size), jnp.float32)],
        compiler_params=pltpu.CompilerParams(vmem_limit_bytes=10 * MIB),
        cost_estimate=LIGHT,
        name="forward_parts",
    )(me, cols, hidden, weights)


def put_shards(me, shards, given, section, sem):
    ahead = 1 - 2 * lax.rem(me, 2)
    for act in ("start", "wait"):
        for number, (step, side, piece, pieces, ref) in enumerate(given):
            shard = me + ahead * (step if side == 0 else -step)
            rows = ref.shape[0]

            @pl.when((shard >= 0) & (shard < shards))
            def _(act=act, number=number, piece=piece, pieces=pieces, ref=ref, shard=shard, rows=rows):
                to = section.at[pl.ds(pl.multiple_of((shard * pieces + piece) * rows, rows), rows), :]
                getattr(pltpu.make_async_copy(ref, to, sem.at[number]), act)()


def section_kernel(shards, labels, me_ref, *refs):
    *given, section, sem = refs
    put_shards(me_ref[0], shards, [(*a, r) for a, r in zip(labels, given)], section, sem)


def start_section(me, shards, given):
    labels, arrays = [a for a, _ in given], [a for _, a in given]
    rows, width = arrays[0].shape
    return pl.pallas_call(
        functools.partial(section_kernel, shards, labels),
        out_shape=jax.ShapeDtypeStruct((rows * labels[0][3] * shards, width), jnp.bfloat16),
        in_specs=[IN_SMEM] + [ANYWHERE] * len(arrays),
        out_specs=IN_VMEM,
        scratch_shapes=[pltpu.SemaphoreType.DMA((len(arrays),))],
        compiler_params=pltpu.CompilerParams(vmem_limit_bytes=4 * MIB),
        cost_estimate=LIGHT,
        name="start_section",
    )(me, *arrays)


def mix_kernel(own_ref, mate_ref, mixed_ref):
    count = own_ref.shape[0]
    for i in range(count):
        both = own_ref[i].astype(jnp.float32) + mate_ref[i].astype(jnp.float32)
        mixed_ref[pl.program_id(0) * count + i] = ((0.5 * MOMENT_DECAY) * both).astype(jnp.bfloat16)


def mix_momentum(momentum, mate_m, after):
    mate_m, _ = lax.optimization_barrier((mate_m, after))
    row_blocks, block_size, width = momentum.shape
    count = row_blocks // 2 if row_blocks % 2 == 0 else 1
    window = pl.BlockSpec((count, block_size, width), lambda i: (i, 0, 0))
    return pl.pallas_call(
        mix_kernel,
        out_shape=jax.ShapeDtypeStruct(momentum.shape, jnp.bfloat16),
        grid=(row_blocks // count,),
        in_specs=[window, window],
        out_specs=IN_VMEM,
        compiler_params=pltpu.CompilerParams(vmem_limit_bytes=10 * MIB),
        cost_estimate=LIGHT,
        name="mix_momentum",
    )(momentum, mate_m)


def update_kernel(scale, shards, first, count, labels, me_ref, cols_ref, hid_ref, w_ref, mate_w_ref, mixed_ref, section, *refs):
    late, (held_w, held_m, sem) = refs[: len(labels)], refs[-3:]
    new_w_ref, new_m_ref = refs[-6:-4] if labels else refs[-5:-3]
    block_size = w_ref.shape[1]
    per_row = w_ref.shape[2] // block_size
    if labels:
        section = refs[-4]
        put_shards(me_ref[0], shards, [(*a, r) for a, r in zip(labels, late)], section, sem.at[2])

    half = jnp.asarray(0.5, jnp.bfloat16)

    def copies_out(i):
        return [
            pltpu.make_async_copy(held.at[i], new.at[first + i], sem.at[number, i])
            for number, (held, new) in enumerate(((held_w, new_w_ref), (held_m, new_m_ref)))
        ]

    for i in range(count):
        hid = hid_ref[:, i * block_size : (i + 1) * block_size].T
        for k in range(0, per_row, 2):
            selected = []
            for j in range(2):
                col = cols_ref[k + j, first + i]
                selected.append(section[:, pl.ds(pl.multiple_of(col * block_size, block_size), block_size)])
            gradient = scale * jnp.dot(hid, jnp.concatenate(selected, 1), preferred_element_type=jnp.float32)
            at = (slice(None), slice(k * block_size, (k + 2) * block_size))
            own_w, mate_w = w_ref[i, *at], mate_w_ref[i, *at]
            half_gap = (half * (mate_w - own_w)).astype(jnp.float32)
            mean_w = (half * (own_w + mate_w)).astype(jnp.float32)
            corrected = gradient + LAMBDA_DC * gradient * gradient * half_gap
            moment = mixed_ref[i, *at].astype(jnp.float32) + corrected
            held_m[i, *at] = moment.astype(jnp.bfloat16)
            held_w[i, *at] = (mean_w - LEARN_RATE * moment).astype(jnp.bfloat16)
        for copy in copies_out(i):
            copy.start()
    for i in range(count):
        for copy in copies_out(i):
            copy.wait()


def update(me, cols, hidden, weights, mate_w, mixed, section, late, scale, shards, first, count, made):
    block_size, width = mate_w.shape[1:]
    mate_first = first if mate_w.shape[0] == weights.shape[0] else 0
    shape = jax.ShapeDtypeStruct(weights.shape, jnp.bfloat16)
    labels, arrays = [a for a, _ in late], [a for _, a in late]
    aliases = {7 + len(arrays) + i: i for i in range(len(made))}
    if late:
        aliases[6] = 2
    held = pltpu.VMEM((count, block_size, width), jnp.bfloat16)
    window = pl.BlockSpec((count, block_size, width), lambda i: (first // count, 0, 0))
    mates = pl.BlockSpec((count, block_size, width), lambda i: (mate_first // count, 0, 0))
    hid = pl.BlockSpec((hidden.shape[0], count * block_size), lambda i: (0, first // count))
    new = pl.pallas_call(
        functools.partial(update_kernel, scale, shards, first, count, labels),
        out_shape=[shape, shape] + [jax.ShapeDtypeStruct(section.shape, section.dtype)] * bool(late),
        grid=(1,),
        in_specs=[IN_SMEM, IN_SMEM, hid, window, mates, window, IN_VMEM] + [ANYWHERE] * (len(arrays) + len(made)),
        out_specs=[ANYWHERE, ANYWHERE] + [IN_VMEM] * bool(late),
        scratch_shapes=[held, held, pltpu.SemaphoreType.DMA((3, max(count, len(arrays))))],
        input_output_aliases=aliases,
        compiler_params=pltpu.CompilerParams(vmem_limit_bytes=16 * MIB),
        cost_estimate=LIGHT,
        name="update",
    )(me, cols, hidden, weights, mate_w, mixed, section, *arrays, *made)
    return list(new)


def ahead_kernel(scale, first, cols_ref, hid_ref, mixed_ref, section, base_ref, factor_ref):
    count, block_size, width = mixed_ref.shape
    for i in range(count):
        hid = hid_ref[:, i * block_size : (i + 1) * block_size].T
        for k in range(width // block_size):
            col = cols_ref[k, first + i]
            selected = section[:, pl.ds(pl.multiple_of(col * block_size, block_size), block_size)]
            gradient = scale * jnp.dot(hid, selected, preferred_element_type=jnp.float32)
            at = (i, slice(None), slice(k * block_size, (k + 1) * block_size))
            base_ref[at] = mixed_ref[at].astype(jnp.float32) + gradient
            factor_ref[at] = (0.5 * LAMBDA_DC) * gradient * gradient


def update_ahead(cols, hidden, mixed, section, scale, first):
    row_blocks, block_size, width = mixed.shape
    count = row_blocks - first
    window = pl.BlockSpec((count, block_size, width), lambda i: (first // count, 0, 0))
    return pl.pallas_call(
        functools.partial(ahead_kernel, scale, first),
        out_shape=[jax.ShapeDtypeStruct((count, block_size, width), jnp.float32)] * 2,
        grid=(1,),
        in_specs=[
            IN_SMEM,
            pl.BlockSpec((hidden.shape[0], count * block_size), lambda i: (0, first // count)),
            window,
            IN_VMEM,
        ],
        out_specs=[IN_VMEM, IN_VMEM],
        compiler_params=pltpu.CompilerParams(vmem_limit_bytes=8 * MIB),
        cost_estimate=LIGHT,
        name="update_ahead",
    )(cols, hidden, mixed, section)


def finish_kernel(first, w_ref, mate_w_ref, base_ref, factor_ref, *refs):
    new_w_ref, new_m_ref, held_w, held_m, sem = refs[-5:]
    count = w_ref.shape[0]
    half = jnp.asarray(0.5, jnp.bfloat16)
    copies = []

    def send(number, held, new, i):
        copies.append(pltpu.make_async_copy(held.at[i], new.at[first + i], sem.at[number, i]))
        copies[-1].start()

    for i in range(count):
        own_w, mate_w = w_ref[i], mate_w_ref[i]
        moment = base_ref[i] + factor_ref[i] * (mate_w - own_w).astype(jnp.float32)
        held_m[i] = moment.astype(jnp.bfloat16)
        send(1, held_m, new_m_ref, i)
        mean_w = (half * (own_w + mate_w)).astype(jnp.float32)
        held_w[i] = (mean_w - LEARN_RATE * moment).astype(jnp.bfloat16)
        send(0, held_w, new_w_ref, i)
    for copy in copies:
        copy.wait()


def finish_update(weights, mate_w, base, factor, first, made):
    count, block_size, width = mate_w.shape
    held = pltpu.VMEM(mate_w.shape, jnp.bfloat16)
    shape = jax.ShapeDtypeStruct(weights.shape, jnp.bfloat16)
    return pl.pallas_call(
        functools.partial(finish_kernel, first),
        out_shape=[shape, shape],
        grid=(1,),
        in_specs=[pl.BlockSpec(mate_w.shape, lambda i: (first // count, 0, 0))] + [IN_VMEM] * 3 + [ANYWHERE] * 2,
        out_specs=[ANYWHERE, ANYWHERE],
        scratch_shapes=[held, held, pltpu.SemaphoreType.DMA((2, count))],
        input_output_aliases={4: 0, 5: 1},
        compiler_params=pltpu.CompilerParams(vmem_limit_bytes=8 * MIB),
        cost_estimate=LIGHT,
        name="finish_update",
    )(weights, mate_w, base, factor, *made)


def add_kernel(*refs):
    (*done, own, got_a, got_b, total, held, sem) = refs
    rows = own.shape[0]
    copies = [
        pltpu.make_async_copy(ref, total.at[pl.ds(h * rows, rows)], sem.at[h]) for h, ref in enumerate((*done, held))
    ]
    for copy in copies[:-1]:
        copy.start()
    for r in range(0, rows, 16):
        at = slice(r, r + 16)
        held[at, :] = sum(t[at, :].astype(jnp.float32) for t in (own, got_a, got_b)).astype(jnp.bfloat16)
    copies[-1].start()
    for copy in copies:
        copy.wait()


def add_up(done, terms):
    rows, width = terms[0].shape
    count = len(done) + 1
    return pl.pallas_call(
        add_kernel,
        out_shape=jax.ShapeDtypeStruct((rows * count, width), jnp.bfloat16),
        in_specs=[ANYWHERE] * len(done) + [IN_VMEM] * 3,
        out_specs=pl.BlockSpec(memory_space=pltpu.HBM),
        scratch_shapes=[pltpu.VMEM((rows, width), jnp.bfloat16), pltpu.SemaphoreType.DMA((count,))],
        compiler_params=pltpu.CompilerParams(vmem_limit_bytes=4 * MIB),
        cost_estimate=LIGHT,
        name="add_up",
    )(*done, *terms)


def exchange(value, parity, shards):
    pairs = [(i, i + 1) for i in range(parity, shards - 1, 2)]
    return lax.ppermute(value, "tensor", pairs + [(j, i) for i, j in pairs])


def gather_and_scatter(own, make_parts, after_phase, along, shards, pieces):
    rows = own.shape[0] // pieces
    whole = [exchange(own, side, shards) for side in (0, 1)]
    parts = make_parts()
    whole, parts, along[0] = lax.optimization_barrier((whole, parts, along[0]))
    given = [((0, 0, 0, 1), own)] + [((1, side, 0, 1), whole[side]) for side in (0, 1)]
    got = [[a[h * rows : (h + 1) * rows] for a in whole] for h in range(pieces)]
    for p in range(1, shards):
        for h in range(pieces):
            if p > 1:
                got[h], parts, along[p - 1] = lax.optimization_barrier((got[h], parts, along[p - 1]))
                given += [((p, side, h, pieces), got[h][side]) for side in (1, 0)]
            part = [parts[(2 * p - 1 + side) * pieces + h] for side in (0, 1)]
            got[h] = [exchange(got[h][1 - side] + part[side], side, shards) for side in (0, 1)]
        result = after_phase(p, given, parts)
    totals = []
    for h in range(pieces):
        result, along[shards - 1], got[h] = lax.optimization_barrier((result, along[shards - 1], got[h]))
        if h < pieces - 1:
            totals.append(sum(a.astype(jnp.float32) for a in (parts[h], *got[h])).astype(jnp.bfloat16))
            result, totals = lax.optimization_barrier((result, totals))
    return result, add_up(totals, (parts[pieces - 1], *got[-1]))


def step_for(bit, hidden, out_grad, weights, momentum, block_cols):
    shards = lax.axis_size("tensor")
    replicas = lax.axis_size("replica")
    model_width = out_grad.shape[1]
    scale = (4.0 / (hidden.shape[1] * shards)) ** 0.5
    me = lax.axis_index("tensor").reshape(1).astype(jnp.int32)
    cols = block_cols.T
    row_blocks = weights.shape[0]
    fixed = (me, cols, hidden, weights)

    def swap(value):
        return lax.ppermute(value, "replica", [(i, i ^ 1 << bit) for i in range(replicas)])

    def forward(pieces):
        return lambda: forward_parts(me, cols, hidden, weights, scale, shards, pieces, model_width)

    along = [[] for _ in range(shards)]
    along[0].append(swap(momentum))
    if bit == 0:
        counted = []

        def parts_then_mix():
            parts = forward(2)()
            along[0][0] = mix_momentum(momentum, along[0][0], parts[0])
            return parts

        def beside(p, given, parts):
            if p == 1:
                behind, _ = lax.optimization_barrier((weights, parts[0]))
                along[shards - 2].append(swap(behind))
            if p == shards - 2:
                counted.append(len(given))
                along[p].append(start_section(me, shards, given))
            if p == shards - 1:
                (count,), (mixed,), (mate_w, section) = counted, along[0], along[shards - 2]
                late = given[count:]
                return update(*fixed, mate_w, mixed, section, late, scale, shards, 0, row_blocks, [])[:2]

        made, outputs = gather_and_scatter(out_grad, parts_then_mix, beside, along, shards, 2)
        return outputs, *made

    cut = row_blocks - rows_per_step(row_blocks)
    head, tail = swap(weights[:cut]), swap(weights[cut:])

    def gathered(p, given, parts):
        return start_section(me, shards, given) if p == shards - 1 else None

    section, outputs = gather_and_scatter(out_grad, forward(1), gathered, along, shards, 1)
    mixed = mix_momentum(momentum, along[0][0], section)
    ahead = update_ahead(cols, hidden, mixed, section, scale, cut)
    head, outputs, ahead = lax.optimization_barrier((head, outputs, ahead))
    made = update(*fixed, head, mixed, section, [], scale, shards, 0, cut, [])
    made = finish_update(weights, tail, *ahead, cut, made)
    return outputs, *made


def body(hidden, out_grad, weights, momentum, block_cols, step_number):
    levels = lax.axis_size("replica").bit_length() - 1
    outputs, new_w, new_m = lax.switch(
        lax.rem(step_number[0], levels),
        [functools.partial(step_for, bit) for bit in range(levels)],
        hidden,
        out_grad,
        weights[0],
        momentum[0],
        block_cols,
    )
    return outputs, new_w[None], new_m[None]


def solution(mesh):
    return jax.shard_map(
        body,
        mesh=mesh,
        in_specs=(
            P("replica", "tensor"),
            P(("replica", "tensor"), None),
            P("replica", "tensor", None, None),
            P("replica", "tensor", None, None),
            P("tensor", None),
            P(),
        ),
        out_specs=(
            P(("replica", "tensor"), None),
            P("replica", "tensor", None, None),
            P("replica", "tensor", None, None),
        ),
        check_vma=False,
    )
```
